1024 devices in a mesh: grp: 64 (over y, x), loc: 16 (over z, core).
Axes of the slice: x: 8, y: 8, z: 8, core: 2. Of those that a mesh axis runs over, the one named last changes fastest.
Arguments:
- token_grads: bfloat16 [131072, 2048], P(('grp', 'loc')), may hold values from -6 to 6
- owner_loc: int32 [131072, 2], P(('grp', 'loc')), may hold values from 0 to 15, as said below
- owner_group: int32 [131072, 2], P(('grp', 'loc')), may hold values from 0 to 63, as said below
- owner_row: int32 [131072, 2], P(('grp', 'loc')), may hold values from 0 to 31, as said below
- embed_table: float32 [32768, 2048], P(('grp', 'loc')), may hold values from -6 to 6
- first_moment: float32 [32768, 2048], P(('grp', 'loc')), may hold values from -4 to 4
- second_moment: float32 [32768, 2048], P(('grp', 'loc')), may hold values from 0.01 to 1
Outputs:
- new_table: float32 [32768, 2048], P(('grp', 'loc'))
- new_first: float32 [32768, 2048], P(('grp', 'loc'))
- new_second: float32 [32768, 2048], P(('grp', 'loc'))
The draws below stay inside these ranges and needn't reach their ends.
Inputs may be any that keep to these rules, and one draw needn't show every extreme that they name: `owner_loc`: among the 256 entries of one device, no value appears more than 32 times, and one value appears exactly 32 times. Among all entries held by the devices of one grp index that share one owner_loc value, no owner_group value appears more than 8 times, and one appears exactly 8 times. Among all entries held by the devices of one grp index that share one owner_loc value and one owner_group value, at most 4 distinct owner_row values appear, and exactly 4 in some.
All inputs are finite; a program needn't handle non-finite values.
Results may differ from the reference program's by a relative error of at most 0.0029.
Values may be sent and summed in bfloat16 or wider, within the bound.
No kernel may reach another device: no remote copies, remote signals or barrier semaphores. Data moves between devices by JAX's collectives and lax.ppermute only.
A program may use at most 32 MiB of HBM per device.

```python
import math
import jax
import jax.numpy as jnp
from jax import lax

D = 2048
TOK_DEV = 128
ROWS_DEV = 32
ADAM_STEP = 100
TOKENS = 131072
TABLE_ROWS = 32768
GROUP_TOKENS = 2048
N_GRP = 64
N_LOC = 16


def routing(key):
    dev_count = N_GRP * N_LOC
    entries = 2 * TOK_DEV
    total = dev_count * entries
    cap_loc = 4 * TOK_DEV // N_LOC
    cap_raw = max(4, 4 * TOK_DEV // N_GRP)
    cap_grp = max(2, cap_raw // 2)
    keys = jax.random.split(key, 4)
    hot_loc = jax.random.randint(keys[0], (dev_count, 1), 0, N_LOC)
    scores = jax.random.randint(keys[1], (dev_count, entries), 0, 2 ** 20) * entries + jnp.arange(entries, dtype=jnp.int32)[None, :]
    position = jnp.argsort(jnp.argsort(scores, axis=1), axis=1).astype(jnp.int32)
    spread = (hot_loc + 1 + (position - cap_loc) % (N_LOC - 1)) % N_LOC
    dest_loc = jnp.where(position < cap_loc, hot_loc, spread).astype(jnp.int32)
    dev_group = (jnp.arange(dev_count, dtype=jnp.int32) // N_LOC)[:, None]
    klass = (dev_group * N_LOC + dest_loc).reshape(total)
    index = jnp.arange(total, dtype=jnp.int32)
    order = jnp.argsort(klass * total + index).astype(jnp.int32)
    sorted_class = klass[order]
    first = jnp.searchsorted(sorted_class, sorted_class, side='left').astype(jnp.int32)
    rank = jnp.zeros((total,), jnp.int32).at[order].set(index - first)
    hot_group = jax.random.randint(keys[2], (dev_count,), 0, N_GRP)[klass]
    beyond = rank - cap_raw
    others = (hot_group + 1 + beyond % (N_GRP - 1)) % N_GRP
    is_hot = rank < cap_raw
    dest_group = jnp.where(is_hot, hot_group, others).astype(jnp.int32)
    sub_rank = jnp.where(is_hot, rank, beyond // (N_GRP - 1))
    base_table = jax.random.randint(keys[3], (dev_count, N_GRP), 0, ROWS_DEV)
    base = base_table[klass, dest_group]
    dest_row = ((base + sub_rank % cap_grp) % ROWS_DEV).astype(jnp.int32)
    return (dest_loc.reshape(TOKENS, 2), dest_group.reshape(TOKENS, 2), dest_row.reshape(TOKENS, 2))


def draw_owner_loc(key, part):
    return routing(key)[0]


def draw_owner_group(key, part):
    return routing(key)[1]


def draw_owner_row(key, part):
    return routing(key)[2]


def steps_of(rng, extent, cuts, low, largest):
    factor_of = 1.0
    for dim, shards_of in cuts:
        steps = jax.random.uniform(jax.random.fold_in(jax.random.fold_in(rng, 6), dim), (shards_of,), jnp.float32, low / len(cuts), largest / len(cuts))
        factor_of = factor_of * jnp.repeat(jnp.exp(steps), extent[dim] // shards_of).reshape((-1,) + (1,) * (len(extent) - 1 - dim))
    return factor_of


def bell_draw(key, shape, scale, bound, pieces=(), kind=jnp.bfloat16):
    gain = steps_of(key, shape, pieces, -0.22, 0.18) if pieces else 1.0
    drawn = jax.random.normal(key, shape, jnp.float32) * scale * gain
    return jnp.minimum(jnp.maximum(drawn, -bound), bound).astype(kind)


def setup_inputs(seed: int = 0) -> dict:
    streams_of = jax.random.split(jax.random.key(seed), 8)
    return {
        "token_grads": bell_draw(streams_of[0], (TOKENS, D), 1.0, 6.0, ((0, 1024),)),
        "owner_loc": draw_owner_loc(jax.random.fold_in(streams_of[7], 71), 0),
        "owner_group": draw_owner_group(jax.random.fold_in(streams_of[7], 71), 0),
        "owner_row": draw_owner_row(jax.random.fold_in(streams_of[7], 71), 0),
        "embed_table": bell_draw(streams_of[4], (TABLE_ROWS, D), 1.0, 6.0, ((0, 1024),), jnp.float32),
        "first_moment": bell_draw(streams_of[5], (TABLE_ROWS, D), 0.5, 4.0, ((0, 1024),), jnp.float32),
        "second_moment": jnp.clip(jnp.exp(math.log(1.0) - 4.6051702 * jax.random.uniform(streams_of[6], (TABLE_ROWS, D), jnp.float32) ** steps_of(streams_of[6], (TABLE_ROWS, D), ((0, 1024),), -0.2, 0.2)), 0.01, 1.0),
    }


beta_one = 0.9
beta_two = 0.999
learn_rate = 0.01
epsilon = 1e-08

def adam_rows(embed_table, first_moment, second_moment, row_grad, touched):
    corr_one = 1.0 - beta_one ** ADAM_STEP
    corr_two = 1.0 - beta_two ** ADAM_STEP
    first_next = beta_one * first_moment + (1.0 - beta_one) * row_grad
    second_next = beta_two * second_moment + (1.0 - beta_two) * row_grad * row_grad
    update = learn_rate * (first_next / corr_one) / (jnp.sqrt(second_next / corr_two) + epsilon)
    table_next = embed_table - update
    mask = touched[:, None]
    return (jnp.where(mask, table_next, embed_table), jnp.where(mask, first_next, first_moment), jnp.where(mask, second_next, second_moment))

def reference(token_grads, owner_loc, owner_group, owner_row, embed_table, first_moment, second_moment):
    row_ids = ((owner_group * N_LOC + owner_loc) * ROWS_DEV + owner_row).astype(jnp.int32)
    group_entries = 2 * GROUP_TOKENS
    ids_by_group = row_ids.reshape(N_GRP, group_entries)
    grads_by_group = token_grads.reshape(N_GRP, GROUP_TOKENS, D)

    def one_group(carry, inputs):
        ids, grads = inputs
        same = ids[:, None] == ids[None, :]
        first = jnp.argmax(same, axis=1).astype(jnp.int32)
        entry_grads = jnp.repeat(grads.astype(jnp.float32), 2, axis=0)
        partial_value = jax.ops.segment_sum(entry_grads, first, num_segments=group_entries)
        rounded = lax.optimization_barrier(partial_value.astype(jnp.bfloat16)).astype(jnp.float32)
        return (carry.at[ids].add(rounded), None)
    row_grad, _ = lax.scan(one_group, jnp.zeros((TABLE_ROWS, D), jnp.float32), (ids_by_group, grads_by_group))
    ones = jnp.ones((row_ids.shape[0],), jnp.int32)
    hits = jax.ops.segment_sum(ones, row_ids[:, 0], num_segments=TABLE_ROWS)
    hits = hits + jax.ops.segment_sum(ones, row_ids[:, 1], num_segments=TABLE_ROWS)
    new_table, new_first, new_second = adam_rows(embed_table, first_moment, second_moment, row_grad, hits > 0)
    return (new_table, new_first, new_second)
```

```python
import functools

import jax
import jax.numpy as jnp
from jax import lax
from jax.experimental import pallas as pl
from jax.experimental.pallas import tpu as pltpu
from jax.sharding import PartitionSpec as P

ADAM_STEP = 100
SLOTS = 4

beta_one = 0.9
beta_two = 0.999
learn_rate = 0.01
epsilon = 1e-08


def iota(shape, dim):
    return lax.broadcasted_iota(jnp.int32, shape, dim)


def plan_kernel(groups, locs, rows, me_ref, ids_ref, select_ref, tag_ref):
    me = me_ref[0]
    slots = groups * SLOTS
    ids = ids_ref[...]
    tokens = ids.shape[1]
    row = ids % rows
    owner = ids // rows
    group = jnp.where(owner % locs == me, owner // locs, -1)
    present = jnp.zeros((groups, rows), jnp.float32)
    for i in range(ids.shape[0]):
        in_group = jnp.where(group[i : i + 1] == iota((groups, tokens), 0), 1.0, 0.0)
        in_row = jnp.where(row[i : i + 1] == iota((rows, tokens), 0), 1.0, 0.0)
        present += lax.dot_general(
            in_group.astype(jnp.bfloat16),
            in_row.astype(jnp.bfloat16),
            (((1,), (1,)), ((), ())),
            preferred_element_type=jnp.float32,
        )
    hit = jnp.where(present > 0.5, 1.0, 0.0).astype(jnp.bfloat16)
    below = jnp.where(iota((rows, rows), 0) < iota((rows, rows), 1), 1.0, 0.0).astype(jnp.bfloat16)
    spread = jnp.where(iota((slots, groups), 0) // SLOTS == iota((slots, groups), 1), 1.0, 0.0)
    hits = jnp.dot(spread.astype(jnp.bfloat16), hit, preferred_element_type=jnp.float32)
    rank = jnp.dot(hits.astype(jnp.bfloat16), below, preferred_element_type=jnp.float32)
    turn = (iota((slots, rows), 0) % SLOTS).astype(jnp.float32)
    mine = (hits > 0.5) & (jnp.abs(rank - turn) < 0.5)
    lane = iota((slots, rows), 1)
    slot_row = jnp.max(jnp.where(mine, lane, -1), axis=1, keepdims=True)
    slot_group = iota((slots, 1), 0) // SLOTS
    slot_id = jnp.where(slot_row >= 0, (slot_group * locs + me) * rows + slot_row, -1)
    for i in range(locs):
        one = jnp.where(ids[2 * i : 2 * i + 1] == slot_id, 1.0, 0.0)
        two = jnp.where(ids[2 * i + 1 : 2 * i + 2] == slot_id, 1.0, 0.0)
        select_ref[:, i * tokens : (i + 1) * tokens] = (one + two).astype(jnp.bfloat16)
    spot = iota((slots, 128), 1)
    placed = jnp.where(
        (spot % SLOTS == iota((slots, 128), 0) % SLOTS) & (spot < 2 * SLOTS), slot_row.astype(jnp.float32), 0.0
    )
    tag = lax.dot_general(
        spread.astype(jnp.bfloat16),
        placed.astype(jnp.bfloat16),
        (((0,), (0,)), ((), ())),
        preferred_element_type=jnp.float32,
    )
    tag_ref[...] = tag.astype(jnp.int32)


def member_kernel(rows, tag_ref, member_ref):
    groups = tag_ref.shape[0]
    wide = groups * 2 * SLOTS
    tag = tag_ref[...].astype(jnp.float32).astype(jnp.bfloat16)
    spread = jnp.where(iota((groups, wide), 1) // (2 * SLOTS) == iota((groups, wide), 0), 1.0, 0.0)
    lanes = lax.dot_general(
        tag,
        spread.astype(jnp.bfloat16),
        (((0,), (0,)), ((), ())),
        preferred_element_type=jnp.float32,
    )[: 2 * SLOTS]
    spot = iota((2 * SLOTS, wide), 1) % (2 * SLOTS)
    line = jnp.sum(jnp.where(iota((2 * SLOTS, wide), 0) == spot, lanes, 0.0), axis=0, keepdims=True)
    same = line.astype(jnp.int32) == iota((rows, wide), 0)
    half = iota((rows, wide), 1) // SLOTS % 2
    for h in range(2):
        member_ref[h] = jnp.where(same & (half == h), 1.0, 0.0).astype(jnp.bfloat16)


def combine_kernel(select_ref, low_ref, high_ref, out_ref):
    select = select_ref[...]
    low = jnp.dot(select, low_ref[...], preferred_element_type=jnp.float32)
    high = jnp.dot(select, high_ref[...], preferred_element_type=jnp.float32)
    slots, width = low.shape
    top = iota((slots, width), 0) % 8 < SLOTS
    even = jnp.where(top, low, pltpu.roll(high, SLOTS, 0))
    odd = jnp.where(top, pltpu.roll(low, slots - SLOTS, 0), high)
    even = even.reshape(slots // 8, 1, 8, width)
    odd = odd.reshape(slots // 8, 1, 8, width)
    both = jnp.concatenate([even, odd], axis=1).reshape(slots // SLOTS, 8, width)
    out_ref[...] = both.astype(jnp.bfloat16)


def adam_kernel(member_ref, landed_ref, table_ref, first_ref, second_ref, t_out, f_out, s_out):
    member = member_ref[0]
    groups, eight, width = landed_ref.shape
    landed = landed_ref[...].reshape(groups * eight, width)
    grad = jnp.dot(member, landed, preferred_element_type=jnp.float32)
    touched = jnp.sum(member.astype(jnp.float32), axis=1, keepdims=True) > 0.5
    corr_one = 1.0 - beta_one**ADAM_STEP
    corr_two = 1.0 - beta_two**ADAM_STEP
    first, second, table = first_ref[...], second_ref[...], table_ref[...]
    first_next = beta_one * first + (1.0 - beta_one) * grad
    second_next = beta_two * second + (1.0 - beta_two) * grad * grad
    update = learn_rate * (first_next / corr_one) / (jnp.sqrt(second_next / corr_two) + epsilon)
    t_out[...] = jnp.where(touched, table - update, table)
    f_out[...] = jnp.where(touched, first_next, first)
    s_out[...] = jnp.where(touched, second_next, second)


VMEM = pl.BlockSpec(memory_space=pltpu.VMEM)


def make_plan(me, ids, groups, locs, rows):
    tokens = ids.shape[1]
    return pl.pallas_call(
        functools.partial(plan_kernel, groups, locs, rows),
        out_shape=(
            jax.ShapeDtypeStruct((groups * SLOTS, locs * tokens), jnp.bfloat16),
            jax.ShapeDtypeStruct((groups, 128), jnp.int32),
        ),
        in_specs=[pl.BlockSpec(memory_space=pltpu.SMEM), VMEM],
        out_specs=(VMEM, VMEM),
        cost_estimate=pl.CostEstimate(flops=20_000_000, bytes_accessed=2_000_000, transcendentals=0),
        compiler_params=pltpu.CompilerParams(vmem_limit_bytes=32 << 20),
    )(me, ids)


def make_member(tag, rows):
    groups = tag.shape[0]
    return pl.pallas_call(
        functools.partial(member_kernel, rows),
        out_shape=jax.ShapeDtypeStruct((2, rows, groups * 2 * SLOTS), jnp.bfloat16),
        in_specs=[VMEM],
        out_specs=VMEM,
        compiler_params=pltpu.CompilerParams(vmem_limit_bytes=32 << 20),
    )(tag)


def combine(select, grads, groups):
    slots, tokens = select.shape
    width = grads.shape[1]
    half = width // 2
    block = 256
    steps = half // block
    return pl.pallas_call(
        combine_kernel,
        grid=(steps,),
        out_shape=jax.ShapeDtypeStruct((groups, 2 * SLOTS, half), jnp.bfloat16),
        in_specs=[
            pl.BlockSpec((slots, tokens), lambda c: (0, 0)),
            pl.BlockSpec((tokens, block), lambda c: (0, c)),
            pl.BlockSpec((tokens, block), lambda c: (0, c + steps)),
        ],
        out_specs=pl.BlockSpec((groups, 2 * SLOTS, block), lambda c: (0, 0, c)),
        compiler_params=pltpu.CompilerParams(vmem_limit_bytes=58 << 20),
    )(select, grads, grads)


def update(member, landed, table, first, second):
    groups, eight, half = landed.shape
    rows, width = table.shape
    block = 512
    steps = half // block
    state = pl.BlockSpec((rows, block), lambda i: (0, i))
    return pl.pallas_call(
        adam_kernel,
        grid=(2 * steps,),
        out_shape=(jax.ShapeDtypeStruct(table.shape, table.dtype),) * 3,
        in_specs=[
            pl.BlockSpec((1, rows, groups * eight), lambda i: (i // steps, 0, 0)),
            pl.BlockSpec((groups, eight, block), lambda i: (0, 0, i % steps)),
            state,
            state,
            state,
        ],
        out_specs=(state, state, state),
        compiler_params=pltpu.CompilerParams(vmem_limit_bytes=32 << 20),
    )(member, landed, table, first, second)


def per_device(
    token_grads, owner_loc, owner_group, owner_row, embed_table, first_moment, second_moment
):
    locs = lax.axis_size("loc")
    groups = lax.axis_size("grp")
    rows = embed_table.shape[0]
    grads = lax.all_gather(token_grads, "loc", axis=0, tiled=True)
    row_id = ((owner_group * locs + owner_loc) * rows + owner_row).T
    ids = lax.all_gather(row_id, "loc", axis=0, tiled=True)
    me = lax.axis_index("loc").astype(jnp.int32).reshape(1)
    select, tag = make_plan(me, ids, groups, locs, rows)
    came = lax.all_to_all(
        tag.reshape(groups, 1, 128), "grp", split_axis=0, concat_axis=0, tiled=True
    ).reshape(groups, 128)
    member = make_member(came, rows)
    sums = combine(select, grads, groups)
    landed = lax.all_to_all(sums, "grp", split_axis=0, concat_axis=0, tiled=True)
    return tuple(update(member, landed, embed_table, first_moment, second_moment))


def solution(mesh):
    rows = P(("grp", "loc"), None)
    return jax.shard_map(
        per_device, mesh=mesh, in_specs=(rows,) * 7, out_specs=(rows,) * 3, check_vma=False
    )
```

```python
import functools

import jax
import jax.numpy as jnp
from jax import lax
from jax.experimental import pallas as pl
from jax.experimental.pallas import tpu as pltpu
from jax.sharding import PartitionSpec as P

ADAM_STEP = 100
LANES = 128
SLOTS = 4
TAG_ONE = 16
TAG_TWO = 8

beta_one = 0.9
beta_two = 0.999
learn_rate = 0.01
epsilon = 1e-08

VMEM = pl.BlockSpec(memory_space=pltpu.VMEM)
SMEM = pl.BlockSpec(memory_space=pltpu.SMEM)
NT = (((1,), (1,)), ((), ()))


def iota(shape, dim):
    return lax.broadcasted_iota(jnp.int32, shape, dim)


def ones(mask):
    return jnp.where(mask, 1.0, 0.0).astype(jnp.bfloat16)


def dot(a, b):
    return jnp.dot(a, b, preferred_element_type=jnp.float32)


def dot_nt(a, b):
    return lax.dot_general(a, b, NT, preferred_element_type=jnp.float32)


def pack_kernel(locs, cap, me_ref, loc_ref, group_ref, row_ref, grads_ref, out_ref):
    tokens, width = grads_ref.shape
    shift = me_ref[0] % (LANES // cap) * cap
    before = ones(iota((tokens, tokens), 0) < iota((tokens, tokens), 1))
    base = jnp.zeros((locs, 1), jnp.float32)
    select = jnp.zeros((locs * cap, tokens), jnp.float32)
    tags = jnp.zeros((locs * TAG_ONE, LANES), jnp.float32)
    kind = iota((locs * TAG_ONE, tokens), 0) % TAG_ONE
    for j in range(2):
        dest = loc_ref[j : j + 1]
        member = jnp.where(dest == iota((locs, tokens), 0), 1.0, 0.0)
        ahead = dot(member.astype(jnp.bfloat16), before) + base
        base += jnp.sum(member, axis=1, keepdims=True)
        rank = jnp.sum(ahead * member, axis=0, keepdims=True).astype(jnp.int32)
        select += jnp.where(dest * cap + rank == iota((locs * cap, tokens), 0), 1.0, 0.0)
        group = (group_ref[j : j + 1] + 1).astype(jnp.float32)
        row = row_ref[j : j + 1].astype(jnp.float32)
        value = jnp.where(kind == 0, group, jnp.where(kind == 1, row, 0.0))
        value = jnp.where(dest == iota((locs * TAG_ONE, tokens), 0) // TAG_ONE, value, 0.0)
        tags += dot_nt(value.astype(jnp.bfloat16), ones(rank + shift == iota((LANES, tokens), 0)))
    select = select.astype(jnp.bfloat16)
    blocks = width // LANES
    out_ref[:, blocks * cap :, :] = tags.reshape(locs, TAG_ONE, LANES).astype(jnp.bfloat16)
    for c in range(0, blocks, 2):
        part = dot(select, grads_ref[:, c * LANES : (c + 2) * LANES]).astype(jnp.bfloat16)
        for i in range(2):
            piece = part[:, i * LANES : (i + 1) * LANES].reshape(locs, cap, LANES)
            out_ref[:, (c + i) * cap : (c + i + 1) * cap, :] = piece


def combine_kernel(groups, rows, cap, me_ref, came_ref, out_ref):
    locs = came_ref.shape[0]
    blocks = (came_ref.shape[1] - TAG_ONE) // cap
    lines = locs * cap // LANES
    each = locs // lines
    slots = groups * SLOTS
    tags = came_ref[:, blocks * cap :, :].reshape(locs * TAG_ONE, LANES)
    shape = (2 * lines, locs * TAG_ONE)
    source, kind = iota(shape, 1) // TAG_ONE, iota(shape, 1) % TAG_ONE
    pick = ones((source // each == iota(shape, 0) % lines) & (kind == iota(shape, 0) // lines))
    tags = dot(pick, tags).astype(jnp.int32)
    group, row = tags[:lines] - 1, tags[lines:]
    present = jnp.zeros((groups, rows), jnp.float32)
    for q in range(lines):
        in_group = ones(group[q : q + 1] == iota((groups, LANES), 0))
        in_row = ones(row[q : q + 1] == iota((rows, LANES), 0))
        present += dot_nt(in_group, in_row)
    below = ones(iota((rows, rows), 0) < iota((rows, rows), 1))
    spread = ones(iota((slots, groups), 0) // SLOTS == iota((slots, groups), 1))
    hits = dot(spread, ones(present > 0.5))
    rank = dot(hits.astype(jnp.bfloat16), below).astype(jnp.int32)
    mine = (hits > 0.5) & (rank == iota((slots, rows), 0) % SLOTS)
    slot_row = jnp.max(jnp.where(mine, iota((slots, rows), 1), -1), axis=1, keepdims=True)
    code = jnp.where(slot_row >= 0, iota((slots, 1), 0) // SLOTS * rows + slot_row, -1)
    select = jnp.concatenate(
        [ones(group[q : q + 1] * rows + row[q : q + 1] == code) for q in range(lines)], axis=1
    )
    lane = iota((slots, LANES), 1)
    mark = (lane // 16 == me_ref[0] % 8) & (lane % SLOTS == iota((slots, LANES), 0) % SLOTS)
    mark = jnp.where(mark, (slot_row + 1).astype(jnp.float32), 0.0).astype(jnp.bfloat16)
    shape = (groups * TAG_TWO, slots)
    place = ones((iota(shape, 0) == iota(shape, 1) // SLOTS * TAG_TWO))
    tail = dot(place, mark).reshape(groups, TAG_TWO, LANES)
    out_ref[:, blocks * SLOTS :, :] = tail.astype(jnp.bfloat16)
    top = iota((slots, LANES), 0) % 8 < SLOTS
    for c in range(0, blocks, 4):
        pairs = []
        for b in (c, c + 2):
            part = jnp.concatenate(
                [came_ref[:, i * cap : (i + 1) * cap, :].reshape(locs * cap, LANES) for i in (b, b + 1)], axis=1
            )
            part = dot(select, part)
            low, high = part[:, :LANES], part[:, LANES:]
            even = jnp.where(top, low, pltpu.roll(high, SLOTS, 0)).reshape(slots // 8, 1, 8, LANES)
            odd = jnp.where(top, pltpu.roll(low, slots - SLOTS, 0), high).reshape(slots // 8, 1, 8, LANES)
            pairs.append(jnp.concatenate([even, odd], axis=1).reshape(groups, 8, LANES))
        out_ref[:, c * SLOTS : (c + 4) * SLOTS, :] = jnp.concatenate(pairs, axis=1).astype(jnp.bfloat16)


def update_kernel(landed_ref, table_ref, first_ref, second_ref, t_out, f_out, s_out):
    groups = landed_ref.shape[0]
    rows, width = table_ref.shape
    blocks = width // LANES
    lines = groups // 8
    tags = landed_ref[:, blocks * SLOTS :, :].astype(jnp.float32).reshape(groups * TAG_TWO, LANES)
    shape = (lines, groups * TAG_TWO)
    source, kind = iota(shape, 1) // TAG_TWO, iota(shape, 1) % TAG_TWO
    pick = ones((source // 8 == iota(shape, 0)) & (kind == 0))
    tags = dot(pick, tags.astype(jnp.bfloat16)).astype(jnp.int32) - 1
    shape = (4 * rows, LANES)
    target = iota(shape, 0) % rows
    same_block = iota(shape, 0) // rows == iota(shape, 1) % 16 // SLOTS
    member = jnp.concatenate(
        [ones((tags[i : i + 1] == target) & same_block) for i in range(lines)], axis=1
    )
    touched = jnp.max(member[:rows].astype(jnp.float32), axis=1, keepdims=True) > 0.5
    corr_one = 1.0 - beta_one**ADAM_STEP
    corr_two = 1.0 - beta_two**ADAM_STEP
    for c in range(0, blocks, 8):
        part = jnp.concatenate(
            [
                landed_ref[:, i * SLOTS : (i + 4) * SLOTS, :].reshape(groups * 4 * SLOTS, LANES)
                for i in (c, c + 4)
            ],
            axis=1,
        )
        part = dot(member, part)
        for i in range(8):
            grad = part[i % 4 * rows : (i % 4 + 1) * rows, i // 4 * LANES : (i // 4 + 1) * LANES]
            at = slice((c + i) * LANES, (c + i + 1) * LANES)
            first, second, table = first_ref[:, at], second_ref[:, at], table_ref[:, at]
            first_next = beta_one * first + (1.0 - beta_one) * grad
            second_next = beta_two * second + (1.0 - beta_two) * grad * grad
            update = learn_rate * (first_next / corr_one) / (jnp.sqrt(second_next / corr_two) + epsilon)
            t_out[:, at] = jnp.where(touched, table - update, table)
            f_out[:, at] = jnp.where(touched, first_next, first)
            s_out[:, at] = jnp.where(touched, second_next, second)


PARAMS = pltpu.CompilerParams(vmem_limit_bytes=32 << 20)
WIDE = pltpu.CompilerParams(vmem_limit_bytes=60 << 20)


def pack(me, dest, group, row, grads, locs, cap):
    width = grads.shape[1]
    shape = (locs, width // LANES * cap + TAG_ONE, LANES)
    return pl.pallas_call(
        functools.partial(pack_kernel, locs, cap),
        out_shape=jax.ShapeDtypeStruct(shape, jnp.bfloat16),
        in_specs=[SMEM, VMEM, VMEM, VMEM, VMEM],
        out_specs=VMEM,
        compiler_params=WIDE,
    )(me, dest, group, row, grads)


def combine(me, came, groups, rows, cap):
    blocks = (came.shape[1] - TAG_ONE) // cap
    shape = (groups, blocks * SLOTS + TAG_TWO, LANES)
    return pl.pallas_call(
        functools.partial(combine_kernel, groups, rows, cap),
        out_shape=jax.ShapeDtypeStruct(shape, jnp.bfloat16),
        in_specs=[SMEM, VMEM],
        out_specs=VMEM,
        compiler_params=PARAMS,
    )(me, came)


def update(landed, table, first, second):
    return pl.pallas_call(
        update_kernel,
        out_shape=(jax.ShapeDtypeStruct(table.shape, table.dtype),) * 3,
        in_specs=[VMEM] * 4,
        out_specs=(VMEM,) * 3,
        compiler_params=PARAMS,
    )(landed, table, first, second)


def per_device(
    token_grads, owner_loc, owner_group, owner_row, embed_table, first_moment, second_moment
):
    locs = lax.axis_size("loc")
    groups = lax.axis_size("grp")
    rows = embed_table.shape[0]
    cap = 4 * token_grads.shape[0] // locs
    at_loc = lax.axis_index("loc").astype(jnp.int32).reshape(1)
    at_group = lax.axis_index("grp").astype(jnp.int32).reshape(1)
    packed = pack(at_loc, owner_loc.T, owner_group.T, owner_row.T, token_grads, locs, cap)
    came = lax.all_to_all(packed, "loc", split_axis=0, concat_axis=0, tiled=True)
    sums = combine(at_group, came, groups, rows, cap)
    landed = lax.all_to_all(sums, "grp", split_axis=0, concat_axis=0, tiled=True)
    return tuple(update(landed, embed_table, first_moment, second_moment))


def solution(mesh):
    rows = P(("grp", "loc"), None)
    return jax.shard_map(
        per_device, mesh=mesh, in_specs=(rows,) * 7, out_specs=(rows,) * 3, check_vma=False
    )
```

```python
import functools

import jax
import jax.numpy as jnp
from jax import lax
from jax.experimental import pallas as pl
from jax.experimental.pallas import tpu as pltpu
from jax.sharding import PartitionSpec as P

ADAM_STEP = 100
LANES = 128
SLOTS = 4
TAG_ONE = 16
HALVES = 2
TAG_TWO = 8

beta_one = 0.9
beta_two = 0.999
learn_rate = 0.01
epsilon = 1e-08

VMEM = pl.BlockSpec(memory_space=pltpu.VMEM)
SMEM = pl.BlockSpec(memory_space=pltpu.SMEM)
NT = (((1,), (1,)), ((), ()))


def iota(shape, dim):
    return lax.broadcasted_iota(jnp.int32, shape, dim)


def ones(mask):
    return jnp.where(mask, 1.0, 0.0).astype(jnp.bfloat16)


def dot(a, b):
    return jnp.dot(a, b, preferred_element_type=jnp.float32)


def dot_nt(a, b):
    return lax.dot_general(a, b, NT, preferred_element_type=jnp.float32)


def pack_kernel(chips, me_ref, own_ids_ref, pair_ids_ref, own_ref, pair_ref, *outs):
    tokens, width = own_ref.shape
    full = LANES // 2
    part = full // 2
    far = chips // 2
    chip, core = me_ref[0] // 2, me_ref[0] % 2
    before = ones(iota((tokens, tokens), 0) < iota((tokens, tokens), 1))
    base = jnp.zeros((chips, 1), jnp.float32)
    tags = jnp.zeros((chips * TAG_ONE, LANES), jnp.float32)
    kind = iota((chips * TAG_ONE, tokens), 0) % TAG_ONE
    selects = []
    for ids in (own_ids_ref, pair_ids_ref):
        select = jnp.zeros((chips * full, tokens), jnp.float32)
        for j in range(2):
            dest = ids[j : j + 1]
            step = jnp.where(dest % 2 == core, (dest // 2 - chip + chips) % chips, -1)
            member = jnp.where(step == iota((chips, tokens), 0), 1.0, 0.0)
            ahead = dot(member.astype(jnp.bfloat16), before) + base
            base += jnp.sum(member, axis=1, keepdims=True)
            rank = jnp.sum(ahead * member, axis=0, keepdims=True).astype(jnp.int32)
            select += jnp.where(step * full + rank == iota((chips * full, tokens), 0), 1.0, 0.0)
            group = (ids[2 + j : 3 + j] + 1).astype(jnp.float32)
            row = ids[4 + j : 5 + j].astype(jnp.float32)
            value = jnp.where(kind == 0, group, jnp.where(kind == 1, row, 0.0))
            value = jnp.where(step == iota((chips * TAG_ONE, tokens), 0) // TAG_ONE, value, 0.0)
            spot = rank + step % 2 * full
            tags += dot_nt(value.astype(jnp.bfloat16), ones(spot == iota((LANES, tokens), 0)))
        selects.append(select.astype(jnp.bfloat16))
    select = jnp.concatenate(selects, axis=1)
    tags = tags.astype(jnp.bfloat16)
    blocks = width // LANES // HALVES
    steps = [d for d in range(chips) if d != far]
    for h in range(HALVES):
        into = dict(zip(steps, outs[h * len(steps) : (h + 1) * len(steps)]))
        tail = blocks * full + (TAG_ONE if h == 0 else 0)
        if h == 0:
            for d in steps:
                into[d][blocks * full : tail, :] = tags[d * TAG_ONE : (d + 1) * TAG_ONE]
            for d in (1, chips - 1):
                into[d][tail + blocks * part :, :] = tags[far * TAG_ONE : (far + 1) * TAG_ONE]
        for c in range(0, blocks, 2):
            at = slice((h * blocks + c) * LANES, (h * blocks + c + 2) * LANES)
            grads = jnp.concatenate([own_ref[:, at], pair_ref[:, at]], axis=0)
            packed = dot(select, grads).astype(jnp.bfloat16)
            for i in range(2):
                piece = packed[:, i * LANES : (i + 1) * LANES]
                for d in steps:
                    into[d][(c + i) * full : (c + i + 1) * full, :] = piece[d * full : (d + 1) * full]
                for d, start in ((1, far * full), (chips - 1, far * full + part)):
                    into[d][tail + (c + i) * part : tail + (c + i + 1) * part, :] = piece[start : start + part]


def sum_slots(groups, blocks, select, blocks_of, out_ref):
    slots = groups * SLOTS
    top = iota((slots, LANES), 0) % 8 < SLOTS
    for c in range(0, blocks, 4):
        pairs = []
        for b in (c, c + 2):
            came = dot(select, jnp.concatenate([blocks_of(b), blocks_of(b + 1)], axis=1))
            low, high = came[:, :LANES], came[:, LANES:]
            even = jnp.where(top, low, pltpu.roll(high, SLOTS, 0)).reshape(slots // 8, 1, 8, LANES)
            odd = jnp.where(top, pltpu.roll(low, slots - SLOTS, 0), high).reshape(slots // 8, 1, 8, LANES)
            pairs.append(jnp.concatenate([even, odd], axis=1).reshape(groups, 8, LANES))
        out_ref[:, c * SLOTS : (c + 4) * SLOTS, :] = jnp.concatenate(pairs, axis=1).astype(jnp.bfloat16)


def column_blocks(came):
    full = LANES // 2
    sizes = [full // 2 if i in (len(came) // 2, len(came) // 2 + 1) else full for i in range(len(came))]

    def of(c):
        return jnp.concatenate([r[c * n : (c + 1) * n, :] for r, n in zip(came, sizes)], axis=0)

    return of


def plan_kernel(groups, rows, blocks, me_ref, *refs):
    *came, out_ref, select_ref = refs
    full = LANES // 2
    slots = groups * SLOTS
    chips = len(came) - 1
    far = chips // 2
    tails = []
    for d in range(chips):
        at = blocks * (full // 2 if d == far else full)
        tails.append(came[d if d <= far else d + 1][at : at + TAG_ONE, :])
    tags = jnp.concatenate(tails, axis=0)
    lines = chips // 2
    shape = (2 * lines, chips * TAG_ONE)
    source, kind = iota(shape, 1) // TAG_ONE, iota(shape, 1) % TAG_ONE
    pick = ones((source // 2 == iota(shape, 0) % lines) & (kind == iota(shape, 0) // lines))
    tags = dot(pick, tags).astype(jnp.int32)
    group, row = tags[:lines] - 1, tags[lines:]
    present = jnp.zeros((groups, rows), jnp.float32)
    for q in range(lines):
        in_group = ones(group[q : q + 1] == iota((groups, LANES), 0))
        in_row = ones(row[q : q + 1] == iota((rows, LANES), 0))
        present += dot_nt(in_group, in_row)
    below = ones(iota((rows, rows), 0) < iota((rows, rows), 1))
    spread = ones(iota((slots, groups), 0) // SLOTS == iota((slots, groups), 1))
    hits = dot(spread, ones(present > 0.5))
    rank = dot(hits.astype(jnp.bfloat16), below).astype(jnp.int32)
    mine = (hits > 0.5) & (rank == iota((slots, rows), 0) % SLOTS)
    slot_row = jnp.max(jnp.where(mine, iota((slots, rows), 1), -1), axis=1, keepdims=True)
    code = jnp.where(slot_row >= 0, iota((slots, 1), 0) // SLOTS * rows + slot_row, -1)
    select = jnp.concatenate(
        [ones(group[q : q + 1] * rows + row[q : q + 1] == code) for q in range(lines)], axis=1
    )
    select_ref[...] = select
    lane = iota((slots, LANES), 1)
    mark = (lane // 16 == me_ref[0] % 8) & (lane % SLOTS == iota((slots, LANES), 0) % SLOTS)
    mark = jnp.where(mark, (slot_row + 1).astype(jnp.float32), 0.0).astype(jnp.bfloat16)
    shape = (groups * TAG_TWO, slots)
    place = ones(iota(shape, 0) == iota(shape, 1) // SLOTS * TAG_TWO)
    tail = dot(place, mark).reshape(groups, TAG_TWO, LANES)
    out_ref[:, blocks * SLOTS :, :] = tail.astype(jnp.bfloat16)
    sum_slots(groups, blocks, select, column_blocks(came), out_ref)


def sum_kernel(groups, blocks, select_ref, *refs):
    *came, out_ref = refs
    sum_slots(groups, blocks, select_ref[...], column_blocks(came), out_ref)


def update_kernel(low_ref, high_ref, table_ref, first_ref, second_ref, t_out, f_out, s_out):
    groups = low_ref.shape[0]
    rows, width = table_ref.shape
    blocks = width // LANES
    part_blocks = blocks // HALVES
    lines = groups // 8
    tags = low_ref[:, part_blocks * SLOTS :, :].astype(jnp.float32).reshape(groups * TAG_TWO, LANES)
    shape = (lines, groups * TAG_TWO)
    source, kind = iota(shape, 1) // TAG_TWO, iota(shape, 1) % TAG_TWO
    pick = ones((source // 8 == iota(shape, 0)) & (kind == 0))
    tags = dot(pick, tags.astype(jnp.bfloat16)).astype(jnp.int32) - 1
    shape = (4 * rows, LANES)
    target = iota(shape, 0) % rows
    same_block = iota(shape, 0) // rows == iota(shape, 1) % 16 // SLOTS
    member = jnp.concatenate(
        [ones((tags[i : i + 1] == target) & same_block) for i in range(lines)], axis=1
    )
    touched = jnp.max(member[:rows].astype(jnp.float32), axis=1, keepdims=True) > 0.5
    corr_one = 1.0 - beta_one**ADAM_STEP
    corr_two = 1.0 - beta_two**ADAM_STEP
    for c in range(0, blocks, 8):
        half_ref, off = (low_ref, c) if c < part_blocks else (high_ref, c - part_blocks)
        part = jnp.concatenate(
            [
                half_ref[:, i * SLOTS : (i + 4) * SLOTS, :].reshape(groups * 4 * SLOTS, LANES)
                for i in (off, off + 4)
            ],
            axis=1,
        )
        part = dot(member, part)
        for i in range(8):
            grad = part[i % 4 * rows : (i % 4 + 1) * rows, i // 4 * LANES : (i // 4 + 1) * LANES]
            at = slice((c + i) * LANES, (c + i + 1) * LANES)
            first, second, table = first_ref[:, at], second_ref[:, at], table_ref[:, at]
            first_next = beta_one * first + (1.0 - beta_one) * grad
            second_next = beta_two * second + (1.0 - beta_two) * grad * grad
            update = learn_rate * (first_next / corr_one) / (jnp.sqrt(second_next / corr_two) + epsilon)
            t_out[:, at] = jnp.where(touched, table - update, table)
            f_out[:, at] = jnp.where(touched, first_next, first)
            s_out[:, at] = jnp.where(touched, second_next, second)


PARAMS = pltpu.CompilerParams(vmem_limit_bytes=32 << 20)


def pack(me, own_ids, pair_ids, own, pair, chips):
    full = LANES // 2
    blocks = own.shape[1] // LANES // HALVES
    shapes = []
    for h in range(HALVES):
        tag = TAG_ONE if h == 0 else 0
        for d in range(chips):
            if d != chips // 2:
                length = blocks * full + tag
                if d in (1, chips - 1):
                    length += blocks * full // 2 + tag
                shapes.append(jax.ShapeDtypeStruct((length, LANES), jnp.bfloat16))
    outs = pl.pallas_call(
        functools.partial(pack_kernel, chips),
        out_shape=tuple(shapes),
        in_specs=[SMEM, VMEM, VMEM, VMEM, VMEM],
        out_specs=(VMEM,) * len(shapes),
        compiler_params=PARAMS,
    )(me, own_ids, pair_ids, own, pair)
    return outs[: chips - 1], outs[chips - 1 :]


def travel(packed, chips, length):
    def send(block, up):
        moves = [(c * 2 + i, (c + up) % chips * 2 + i) for c in range(chips) for i in range(2)]
        return lax.ppermute(block, "loc", moves)

    far = chips // 2
    steps = [d for d in range(chips) if d != far]
    block = dict(zip(steps, packed))
    came = {0: block[0]}
    for d in (1, chips - 1, 3, chips - 3, 2, chips - 2):
        came[d] = send(block[d], d)
    parts = [send(came[1][length:], far - 1), send(came[chips - 1][length:], far + 1)]
    return [came[d] for d in range(far)] + parts + [came[d] for d in range(far + 1, chips)]


def first_sums(me, came, groups, rows, blocks):
    slots = groups * SLOTS
    return pl.pallas_call(
        functools.partial(plan_kernel, groups, rows, blocks),
        out_shape=(
            jax.ShapeDtypeStruct((groups, blocks * SLOTS + TAG_TWO, LANES), jnp.bfloat16),
            jax.ShapeDtypeStruct((slots, (len(came) - 1) * LANES // 2), jnp.bfloat16),
        ),
        in_specs=[SMEM] + [VMEM] * len(came),
        out_specs=(VMEM, VMEM),
        compiler_params=PARAMS,
    )(me, *came)


def second_sums(select, came, groups, blocks):
    return pl.pallas_call(
        functools.partial(sum_kernel, groups, blocks),
        out_shape=jax.ShapeDtypeStruct((groups, blocks * SLOTS, LANES), jnp.bfloat16),
        in_specs=[VMEM] * (len(came) + 1),
        out_specs=VMEM,
        compiler_params=PARAMS,
    )(select, *came)


def update(low, high, table, first, second):
    return pl.pallas_call(
        update_kernel,
        out_shape=(jax.ShapeDtypeStruct(table.shape, table.dtype),) * 3,
        in_specs=[VMEM] * 5,
        out_specs=(VMEM,) * 3,
        compiler_params=PARAMS,
    )(low, high, table, first, second)


def per_device(
    token_grads, owner_loc, owner_group, owner_row, embed_table, first_moment, second_moment
):
    locs = lax.axis_size("loc")
    groups = lax.axis_size("grp")
    rows, width = embed_table.shape
    chips = locs // 2
    blocks = width // LANES // HALVES
    at_loc = lax.axis_index("loc").astype(jnp.int32).reshape(1)
    at_group = lax.axis_index("grp").astype(jnp.int32).reshape(1)
    ids = jnp.concatenate([owner_loc.T, owner_group.T, owner_row.T], axis=0)
    swap = [(i, i ^ 1) for i in range(locs)]
    pair_ids = lax.ppermute(ids, "loc", swap)
    pair = lax.ppermute(token_grads, "loc", swap)
    low, high = pack(at_loc, ids, pair_ids, token_grads, pair, chips)
    length = blocks * LANES // 2
    low = travel(low, chips, length + TAG_ONE)
    low, high = lax.optimization_barrier((low, high))
    high = travel(high, chips, length)
    low, select = first_sums(at_group, low, groups, rows, blocks)
    low, high[1], high[-1] = lax.optimization_barrier((low, high[1], high[-1]))
    low = lax.all_to_all(low, "grp", split_axis=0, concat_axis=0, tiled=True)
    low, high[0] = lax.optimization_barrier((low, high[0]))
    high = second_sums(select, high, groups, blocks)
    high = lax.all_to_all(high, "grp", split_axis=0, concat_axis=0, tiled=True)
    return tuple(update(low, high, embed_table, first_moment, second_moment))


def solution(mesh):
    rows = P(("grp", "loc"), None)
    return jax.shard_map(
        per_device, mesh=mesh, in_specs=(rows,) * 7, out_specs=(rows,) * 3, check_vma=False
    )
```

```python
import functools

import jax
import jax.numpy as jnp
from jax import lax
from jax.experimental import pallas as pl
from jax.experimental.pallas import tpu as pltpu
from jax.sharding import PartitionSpec as P

ADAM_STEP = 100
LANES = 128
SLOTS = 4
TAG_ONE = 8
TAG_TWO = 8

beta_one = 0.9
beta_two = 0.999
learn_rate = 0.01
epsilon = 1e-08

VMEM = pl.BlockSpec(memory_space=pltpu.VMEM)
SMEM = pl.BlockSpec(memory_space=pltpu.SMEM)
ANY = pl.BlockSpec(memory_space=pl.ANY)
NT = (((1,), (1,)), ((), ()))


def iota(shape, dim):
    return lax.broadcasted_iota(jnp.int32, shape, dim)


def ones(mask):
    return jnp.where(mask, 1.0, 0.0).astype(jnp.bfloat16)


def dot(a, b):
    return jnp.dot(a, b, preferred_element_type=jnp.float32)


def dot_nt(a, b):
    return lax.dot_general(a, b, NT, preferred_element_type=jnp.float32)


def pack_kernel(locs, cap, me_ref, loc_ref, group_ref, row_ref, from_ref, to_ref, grads_ref, out_ref, sem):
    tokens, width = grads_ref.shape
    read = pltpu.make_async_copy(from_ref, grads_ref, sem.at[0])
    read.start()
    shift = me_ref[0] % (LANES // cap) * cap
    before = ones(iota((tokens, tokens), 0) < iota((tokens, tokens), 1))
    base = jnp.zeros((locs, 1), jnp.float32)
    select = jnp.zeros((locs * cap, tokens), jnp.float32)
    tags = jnp.zeros((locs * TAG_ONE, LANES), jnp.float32)
    kind = iota((locs * TAG_ONE, tokens), 0) % TAG_ONE
    for j in range(2):
        dest = loc_ref[j : j + 1]
        member = jnp.where(dest == iota((locs, tokens), 0), 1.0, 0.0)
        ahead = dot(member.astype(jnp.bfloat16), before) + base
        base += jnp.sum(member, axis=1, keepdims=True)
        rank = jnp.sum(ahead * member, axis=0, keepdims=True).astype(jnp.int32)
        select += jnp.where(dest * cap + rank == iota((locs * cap, tokens), 0), 1.0, 0.0)
        group = (group_ref[j : j + 1] + 1).astype(jnp.float32)
        row = row_ref[j : j + 1].astype(jnp.float32)
        value = jnp.where(kind == 0, group, jnp.where(kind == 1, row, 0.0))
        value = jnp.where(dest == iota((locs * TAG_ONE, tokens), 0) // TAG_ONE, value, 0.0)
        tags += dot_nt(value.astype(jnp.bfloat16), ones(rank + shift == iota((LANES, tokens), 0)))
    select = select.astype(jnp.bfloat16)
    blocks = width // LANES
    out_ref[:, blocks * cap :, :] = tags.reshape(locs, TAG_ONE, LANES).astype(jnp.bfloat16)
    read.wait()
    half = locs // 2
    writes = []
    for h in range(2):
        dests = slice(h * half, (h + 1) * half)
        chosen = select[h * half * cap : (h + 1) * half * cap]
        for c in range(0, blocks, 2):
            part = dot(chosen, grads_ref[:, c * LANES : (c + 2) * LANES]).astype(jnp.bfloat16)
            for i in range(2):
                piece = part[:, i * LANES : (i + 1) * LANES].reshape(half, cap, LANES)
                out_ref[dests, (c + i) * cap : (c + i + 1) * cap, :] = piece
        at = pl.ds(h * half, half)
        writes.append(pltpu.make_async_copy(out_ref.at[at], to_ref.at[at], sem.at[1 + h]))
        writes[-1].start()
    for write in writes:
        write.wait()


def combine_kernel(groups, rows, cap, me_ref, came_ref, out_ref):
    locs = came_ref.shape[0]
    blocks = (came_ref.shape[1] - TAG_ONE) // cap
    lines = locs * cap // LANES
    each = locs // lines
    slots = groups * SLOTS
    tags = came_ref[:, blocks * cap :, :].astype(jnp.float32).reshape(locs * TAG_ONE, LANES)
    shape = (2 * lines, locs * TAG_ONE)
    source, kind = iota(shape, 1) // TAG_ONE, iota(shape, 1) % TAG_ONE
    pick = ones((source // each == iota(shape, 0) % lines) & (kind == iota(shape, 0) // lines))
    tags = dot(pick, tags.astype(jnp.bfloat16)).astype(jnp.int32)
    group, row = tags[:lines] - 1, tags[lines:]
    present = jnp.zeros((groups, rows), jnp.float32)
    for q in range(lines):
        in_group = ones(group[q : q + 1] == iota((groups, LANES), 0))
        in_row = ones(row[q : q + 1] == iota((rows, LANES), 0))
        present += dot_nt(in_group, in_row)
    below = ones(iota((rows, rows), 0) < iota((rows, rows), 1))
    spread = ones(iota((slots, groups), 0) // SLOTS == iota((slots, groups), 1))
    hits = dot(spread, ones(present > 0.5))
    rank = dot(hits.astype(jnp.bfloat16), below).astype(jnp.int32)
    mine = (hits > 0.5) & (rank == iota((slots, rows), 0) % SLOTS)
    slot_row = jnp.max(jnp.where(mine, iota((slots, rows), 1), -1), axis=1, keepdims=True)
    code = jnp.where(slot_row >= 0, iota((slots, 1), 0) // SLOTS * rows + slot_row, -1)
    select = jnp.concatenate(
        [ones(group[q : q + 1] * rows + row[q : q + 1] == code) for q in range(lines)], axis=1
    )
    lane = iota((slots, LANES), 1)
    mark = (lane // 16 == me_ref[0] % 8) & (lane % SLOTS == iota((slots, LANES), 0) % SLOTS)
    mark = jnp.where(mark, (slot_row + 1).astype(jnp.float32), 0.0).astype(jnp.bfloat16)
    shape = (groups * TAG_TWO, slots)
    place = ones((iota(shape, 0) == iota(shape, 1) // SLOTS * TAG_TWO))
    tail = dot(place, mark).reshape(groups, TAG_TWO, LANES)
    out_ref[:, blocks * SLOTS :, :] = tail.astype(jnp.bfloat16)
    top = iota((slots, LANES), 0) % 8 < SLOTS
    for c in range(0, blocks, 4):
        pairs = []
        for b in (c, c + 2):
            part = jnp.concatenate(
                [came_ref[:, i * cap : (i + 1) * cap, :].reshape(locs * cap, LANES) for i in (b, b + 1)], axis=1
            )
            part = dot(select, part)
            low, high = part[:, :LANES], part[:, LANES:]
            even = jnp.where(top, low, pltpu.roll(high, SLOTS, 0)).reshape(slots // 8, 1, 8, LANES)
            odd = jnp.where(top, pltpu.roll(low, slots - SLOTS, 0), high).reshape(slots // 8, 1, 8, LANES)
            pairs.append(jnp.concatenate([even, odd], axis=1).reshape(groups, 8, LANES))
        out_ref[:, c * SLOTS : (c + 4) * SLOTS, :] = jnp.concatenate(pairs, axis=1).astype(jnp.bfloat16)


def update_kernel(landed_ref, table_ref, first_ref, second_ref, t_out, f_out, s_out):
    groups = landed_ref.shape[0]
    rows, width = table_ref.shape
    blocks = width // LANES
    lines = groups // 8
    tags = landed_ref[:, blocks * SLOTS :, :].astype(jnp.float32).reshape(groups * TAG_TWO, LANES)
    shape = (lines, groups * TAG_TWO)
    source, kind = iota(shape, 1) // TAG_TWO, iota(shape, 1) % TAG_TWO
    pick = ones((source // 8 == iota(shape, 0)) & (kind == 0))
    tags = dot(pick, tags.astype(jnp.bfloat16)).astype(jnp.int32) - 1
    shape = (4 * rows, LANES)
    target = iota(shape, 0) % rows
    same_block = iota(shape, 0) // rows == iota(shape, 1) % 16 // SLOTS
    member = jnp.concatenate(
        [ones((tags[i : i + 1] == target) & same_block) for i in range(lines)], axis=1
    )
    touched = jnp.max(member[:rows].astype(jnp.float32), axis=1, keepdims=True) > 0.5
    corr_one = 1.0 - beta_one**ADAM_STEP
    corr_two = 1.0 - beta_two**ADAM_STEP
    for c in range(0, blocks, 8):
        part = jnp.concatenate(
            [
                landed_ref[:, i * SLOTS : (i + 4) * SLOTS, :].reshape(groups * 4 * SLOTS, LANES)
                for i in (c, c + 4)
            ],
            axis=1,
        )
        part = dot(member, part)
        for i in range(8):
            grad = part[i % 4 * rows : (i % 4 + 1) * rows, i // 4 * LANES : (i // 4 + 1) * LANES]
            at = slice((c + i) * LANES, (c + i + 1) * LANES)
            first, second, table = first_ref[:, at], second_ref[:, at], table_ref[:, at]
            first_next = beta_one * first + (1.0 - beta_one) * grad
            second_next = beta_two * second + (1.0 - beta_two) * grad * grad
            update = learn_rate * (first_next / corr_one) / (jnp.sqrt(second_next / corr_two) + epsilon)
            t_out[:, at] = jnp.where(touched, table - update, table)
            f_out[:, at] = jnp.where(touched, first_next, first)
            s_out[:, at] = jnp.where(touched, second_next, second)


PARAMS = pltpu.CompilerParams(vmem_limit_bytes=32 << 20)
WIDE = pltpu.CompilerParams(vmem_limit_bytes=60 << 20)


def pack(me, dest, group, row, grads, locs, cap):
    width = grads.shape[1]
    shape = (locs, width // LANES * cap + TAG_ONE, LANES)
    return pl.pallas_call(
        functools.partial(pack_kernel, locs, cap),
        out_shape=jax.ShapeDtypeStruct(shape, jnp.bfloat16),
        in_specs=[SMEM, VMEM, VMEM, VMEM, ANY],
        out_specs=ANY,
        scratch_shapes=[
            pltpu.VMEM(grads.shape, jnp.bfloat16),
            pltpu.VMEM(shape, jnp.bfloat16),
            pltpu.SemaphoreType.DMA((3,)),
        ],
        compiler_params=WIDE,
    )(me, dest, group, row, grads)


def combine(me, came, groups, rows, cap):
    blocks = (came.shape[1] - TAG_ONE) // cap
    shape = (groups, blocks * SLOTS + TAG_TWO, LANES)
    return pl.pallas_call(
        functools.partial(combine_kernel, groups, rows, cap),
        out_shape=jax.ShapeDtypeStruct(shape, jnp.bfloat16),
        in_specs=[SMEM, VMEM],
        out_specs=VMEM,
        compiler_params=PARAMS,
    )(me, came)


def update(landed, table, first, second):
    return pl.pallas_call(
        update_kernel,
        out_shape=(jax.ShapeDtypeStruct(table.shape, table.dtype),) * 3,
        in_specs=[VMEM] * 4,
        out_specs=(VMEM,) * 3,
        compiler_params=PARAMS,
    )(landed, table, first, second)


def per_device(
    token_grads, owner_loc, owner_group, owner_row, embed_table, first_moment, second_moment
):
    locs = lax.axis_size("loc")
    groups = lax.axis_size("grp")
    rows = embed_table.shape[0]
    cap = 4 * token_grads.shape[0] // locs
    at_loc = lax.axis_index("loc").astype(jnp.int32).reshape(1)
    at_group = lax.axis_index("grp").astype(jnp.int32).reshape(1)
    packed = pack(at_loc, owner_loc.T, owner_group.T, owner_row.T, token_grads, locs, cap)
    came = lax.all_to_all(packed, "loc", split_axis=0, concat_axis=0, tiled=True)
    sums = combine(at_group, came, groups, rows, cap)
    landed = lax.all_to_all(sums, "grp", split_axis=0, concat_axis=0, tiled=True)
    return tuple(update(landed, embed_table, first_moment, second_moment))


def solution(mesh):
    rows = P(("grp", "loc"), None)
    return jax.shard_map(
        per_device, mesh=mesh, in_specs=(rows,) * 7, out_specs=(rows,) * 3, check_vma=False
    )
```

```python
import functools

import jax
import jax.numpy as jnp
from jax import lax
from jax.experimental import pallas as pl
from jax.experimental.pallas import tpu as pltpu
from jax.sharding import PartitionSpec as P

ADAM_STEP = 100
LANES = 128
SLOTS = 4
TAG_ONE = 8
TAG_TWO = 8

beta_one = 0.9
beta_two = 0.999
learn_rate = 0.01
epsilon = 1e-08

VMEM = pl.BlockSpec(memory_space=pltpu.VMEM)
SMEM = pl.BlockSpec(memory_space=pltpu.SMEM)
FAR = pl.BlockSpec(memory_space=pltpu.HBM)
NT = (((1,), (1,)), ((), ()))


def iota(shape, dim):
    return lax.broadcasted_iota(jnp.int32, shape, dim)


def ones(mask):
    return jnp.where(mask, 1.0, 0.0).astype(jnp.bfloat16)


def dot(a, b):
    return jnp.dot(a, b, preferred_element_type=jnp.float32)


def dot_nt(a, b):
    return lax.dot_general(a, b, NT, preferred_element_type=jnp.float32)


def pack_kernel(locs, cap, me_ref, also_ref, loc_from, group_from, row_from, grads_from, out_ref, *scratch):
    *arrays, sem = scratch
    reads = [
        pltpu.make_async_copy(a, b, sem.at[i])
        for i, (a, b) in enumerate(zip((loc_from, group_from, row_from, grads_from), arrays))
    ]
    for read in reads:
        read.start()
    loc_ref, group_ref, row_ref, grads_ref = arrays
    tokens, width = grads_ref.shape
    for read in reads[:3]:
        read.wait()
    shift = me_ref[0] % (LANES // cap) * cap
    before = ones(iota((tokens, tokens), 0) < iota((tokens, tokens), 1))
    base = jnp.zeros((locs, 1), jnp.float32)
    select = jnp.zeros((locs * cap, tokens), jnp.float32)
    tags = jnp.zeros((locs * TAG_ONE, LANES), jnp.float32)
    kind = iota((locs * TAG_ONE, tokens), 0) % TAG_ONE
    for j in range(2):
        dest = loc_ref[j : j + 1]
        member = jnp.where(dest == iota((locs, tokens), 0), 1.0, 0.0)
        ahead = dot(member.astype(jnp.bfloat16), before) + base
        base += jnp.sum(member, axis=1, keepdims=True)
        rank = jnp.sum(ahead * member, axis=0, keepdims=True).astype(jnp.int32)
        select += jnp.where(dest * cap + rank == iota((locs * cap, tokens), 0), 1.0, 0.0)
        group = (group_ref[j : j + 1] + 1).astype(jnp.float32)
        row = row_ref[j : j + 1].astype(jnp.float32)
        value = jnp.where(kind == 0, group, jnp.where(kind == 1, row, 0.0))
        value = jnp.where(dest == iota((locs * TAG_ONE, tokens), 0) // TAG_ONE, value, 0.0)
        tags += dot_nt(value.astype(jnp.bfloat16), ones(rank + shift == iota((LANES, tokens), 0)))
    select = select.astype(jnp.bfloat16)
    blocks = width // LANES
    reads[3].wait()
    out_ref[:, blocks * cap :, :] = tags.reshape(locs, TAG_ONE, LANES).astype(jnp.bfloat16)
    for c in range(0, blocks, 2):
        part = dot(select, grads_ref[:, c * LANES : (c + 2) * LANES]).astype(jnp.bfloat16)
        for i in range(2):
            piece = part[:, i * LANES : (i + 1) * LANES].reshape(locs, cap, LANES)
            out_ref[:, (c + i) * cap : (c + i + 1) * cap, :] = piece


def combine_kernel(groups, rows, cap, me_ref, came_ref, out_ref):
    locs = came_ref.shape[0]
    blocks = (came_ref.shape[1] - TAG_ONE) // cap
    lines = locs * cap // LANES
    each = locs // lines
    slots = groups * SLOTS
    tags = came_ref[:, blocks * cap :, :].astype(jnp.float32).reshape(locs * TAG_ONE, LANES)
    shape = (2 * lines, locs * TAG_ONE)
    source, kind = iota(shape, 1) // TAG_ONE, iota(shape, 1) % TAG_ONE
    pick = ones((source // each == iota(shape, 0) % lines) & (kind == iota(shape, 0) // lines))
    tags = dot(pick, tags.astype(jnp.bfloat16)).astype(jnp.int32)
    group, row = tags[:lines] - 1, tags[lines:]
    present = jnp.zeros((groups, rows), jnp.float32)
    for q in range(lines):
        in_group = ones(group[q : q + 1] == iota((groups, LANES), 0))
        in_row = ones(row[q : q + 1] == iota((rows, LANES), 0))
        present += dot_nt(in_group, in_row)
    below = ones(iota((rows, rows), 0) < iota((rows, rows), 1))
    spread = ones(iota((slots, groups), 0) // SLOTS == iota((slots, groups), 1))
    hits = dot(spread, ones(present > 0.5))
    rank = dot(hits.astype(jnp.bfloat16), below).astype(jnp.int32)
    mine = (hits > 0.5) & (rank == iota((slots, rows), 0) % SLOTS)
    slot_row = jnp.max(jnp.where(mine, iota((slots, rows), 1), -1), axis=1, keepdims=True)
    code = jnp.where(slot_row >= 0, iota((slots, 1), 0) // SLOTS * rows + slot_row, -1)
    select = jnp.concatenate(
        [ones(group[q : q + 1] * rows + row[q : q + 1] == code) for q in range(lines)], axis=1
    )
    lane = iota((slots, LANES), 1)
    mark = (lane // 16 == me_ref[0] % 8) & (lane % SLOTS == iota((slots, LANES), 0) % SLOTS)
    mark = jnp.where(mark, (slot_row + 1).astype(jnp.float32), 0.0).astype(jnp.bfloat16)
    shape = (groups * TAG_TWO, slots)
    place = ones((iota(shape, 0) == iota(shape, 1) // SLOTS * TAG_TWO))
    tail = dot(place, mark).reshape(groups, TAG_TWO, LANES)
    out_ref[:, blocks * SLOTS :, :] = tail.astype(jnp.bfloat16)
    top = iota((slots, LANES), 0) % 8 < SLOTS
    for c in range(0, blocks, 4):
        pairs = []
        for b in (c, c + 2):
            part = jnp.concatenate(
                [came_ref[:, i * cap : (i + 1) * cap, :].reshape(locs * cap, LANES) for i in (b, b + 1)], axis=1
            )
            part = dot(select, part)
            low, high = part[:, :LANES], part[:, LANES:]
            even = jnp.where(top, low, pltpu.roll(high, SLOTS, 0)).reshape(slots // 8, 1, 8, LANES)
            odd = jnp.where(top, pltpu.roll(low, slots - SLOTS, 0), high).reshape(slots // 8, 1, 8, LANES)
            pairs.append(jnp.concatenate([even, odd], axis=1).reshape(groups, 8, LANES))
        out_ref[:, c * SLOTS : (c + 4) * SLOTS, :] = jnp.concatenate(pairs, axis=1).astype(jnp.bfloat16)


def update_kernel(landed_ref, table_ref, first_ref, second_ref, t_out, f_out, s_out):
    groups = landed_ref.shape[0]
    rows, width = table_ref.shape
    blocks = width // LANES
    lines = groups // 8
    tags = landed_ref[:, blocks * SLOTS :, :].astype(jnp.float32).reshape(groups * TAG_TWO, LANES)
    shape = (lines, groups * TAG_TWO)
    source, kind = iota(shape, 1) // TAG_TWO, iota(shape, 1) % TAG_TWO
    pick = ones((source // 8 == iota(shape, 0)) & (kind == 0))
    tags = dot(pick, tags.astype(jnp.bfloat16)).astype(jnp.int32) - 1
    shape = (4 * rows, LANES)
    target = iota(shape, 0) % rows
    same_block = iota(shape, 0) // rows == iota(shape, 1) % 16 // SLOTS
    member = jnp.concatenate(
        [ones((tags[i : i + 1] == target) & same_block) for i in range(lines)], axis=1
    )
    touched = jnp.max(member[:rows].astype(jnp.float32), axis=1, keepdims=True) > 0.5
    corr_one = 1.0 - beta_one**ADAM_STEP
    corr_two = 1.0 - beta_two**ADAM_STEP
    for c in range(0, blocks, 8):
        part = jnp.concatenate(
            [
                landed_ref[:, i * SLOTS : (i + 4) * SLOTS, :].reshape(groups * 4 * SLOTS, LANES)
                for i in (c, c + 4)
            ],
            axis=1,
        )
        part = dot(member, part)
        for i in range(8):
            grad = part[i % 4 * rows : (i % 4 + 1) * rows, i // 4 * LANES : (i // 4 + 1) * LANES]
            at = slice((c + i) * LANES, (c + i + 1) * LANES)
            first, second, table = first_ref[:, at], second_ref[:, at], table_ref[:, at]
            first_next = beta_one * first + (1.0 - beta_one) * grad
            second_next = beta_two * second + (1.0 - beta_two) * grad * grad
            update = learn_rate * (first_next / corr_one) / (jnp.sqrt(second_next / corr_two) + epsilon)
            t_out[:, at] = jnp.where(touched, table - update, table)
            f_out[:, at] = jnp.where(touched, first_next, first)
            s_out[:, at] = jnp.where(touched, second_next, second)


PARAMS = pltpu.CompilerParams(vmem_limit_bytes=32 << 20)
WIDE = pltpu.CompilerParams(vmem_limit_bytes=32 << 20)


def pack(me, also, dest, group, row, grads, locs, cap):
    width = grads.shape[1]
    shape = (locs, width // LANES * cap + TAG_ONE, LANES)
    return pl.pallas_call(
        functools.partial(pack_kernel, locs, cap),
        out_shape=jax.ShapeDtypeStruct(shape, jnp.bfloat16),
        in_specs=[SMEM, SMEM, FAR, FAR, FAR, FAR],
        out_specs=VMEM,
        scratch_shapes=[
            pltpu.VMEM(dest.shape, jnp.int32),
            pltpu.VMEM(dest.shape, jnp.int32),
            pltpu.VMEM(dest.shape, jnp.int32),
            pltpu.VMEM(grads.shape, jnp.bfloat16),
            pltpu.SemaphoreType.DMA((4,)),
        ],
        compiler_params=WIDE,
    )(me, also, *(pltpu.with_memory_space_constraint(a, pltpu.HBM) for a in (dest, group, row, grads)))


def combine(me, came, groups, rows, cap):
    blocks = (came.shape[1] - TAG_ONE) // cap
    shape = (groups, blocks * SLOTS + TAG_TWO, LANES)
    return pl.pallas_call(
        functools.partial(combine_kernel, groups, rows, cap),
        out_shape=jax.ShapeDtypeStruct(shape, jnp.bfloat16),
        in_specs=[SMEM, VMEM],
        out_specs=VMEM,
        compiler_params=PARAMS,
    )(me, came)


def update(landed, table, first, second):
    return pl.pallas_call(
        update_kernel,
        out_shape=(jax.ShapeDtypeStruct(table.shape, table.dtype),) * 3,
        in_specs=[VMEM] * 4,
        out_specs=(VMEM,) * 3,
        compiler_params=PARAMS,
    )(landed, table, first, second)


def per_device(
    token_grads, owner_loc, owner_group, owner_row, embed_table, first_moment, second_moment
):
    locs = lax.axis_size("loc")
    groups = lax.axis_size("grp")
    rows = embed_table.shape[0]
    cap = 4 * token_grads.shape[0] // locs
    at_loc = lax.axis_index("loc").astype(jnp.int32).reshape(1)
    at_group = lax.axis_index("grp").astype(jnp.int32).reshape(1)
    packed = pack(at_loc, at_group, owner_loc.T, owner_group.T, owner_row.T, token_grads, locs, cap)
    came = lax.all_to_all(packed, "loc", split_axis=0, concat_axis=0, tiled=True)
    sums = combine(at_group, came, groups, rows, cap)
    landed = lax.all_to_all(sums, "grp", split_axis=0, concat_axis=0, tiled=True)
    return tuple(update(landed, embed_table, first_moment, second_moment))


def solution(mesh):
    rows = P(("grp", "loc"), None)
    return jax.shard_map(
        per_device, mesh=mesh, in_specs=(rows,) * 7, out_specs=(rows,) * 3, check_vma=False
    )
```

```python
import functools

import jax
import jax.numpy as jnp
from jax import lax
from jax.experimental import pallas as pl
from jax.experimental.pallas import tpu as pltpu
from jax.sharding import PartitionSpec as P

ADAM_STEP = 100
LANES = 128
SLOTS = 4
TAG_ONE = 8
PARTS = 4
TILE = 8

beta_one = 0.9
beta_two = 0.999
learn_rate = 0.01
epsilon = 1e-08

VMEM = pl.BlockSpec(memory_space=pltpu.VMEM)
SMEM = pl.BlockSpec(memory_space=pltpu.SMEM)
ANY = pl.BlockSpec(memory_space=pl.ANY)
NT = (((1,), (1,)), ((), ()))


def iota(shape, dim):
    return lax.broadcasted_iota(jnp.int32, shape, dim)


def ones(mask):
    return jnp.where(mask, 1.0, 0.0).astype(jnp.bfloat16)


def dot(a, b):
    return jnp.dot(a, b, preferred_element_type=jnp.float32)


def dot_nt(a, b):
    return lax.dot_general(a, b, NT, preferred_element_type=jnp.float32)


def pack_kernel(locs, cap, me_ref, loc_ref, group_ref, row_ref, from_ref, to_ref, grads_ref, out_ref, sem):
    tokens, width = grads_ref.shape
    read = pltpu.make_async_copy(from_ref, grads_ref, sem.at[0])
    read.start()
    shift = me_ref[0] % (LANES // cap) * cap
    before = ones(iota((tokens, tokens), 0) < iota((tokens, tokens), 1))
    base = jnp.zeros((locs, 1), jnp.float32)
    select = jnp.zeros((locs * cap, tokens), jnp.float32)
    tags = jnp.zeros((locs * TAG_ONE, LANES), jnp.float32)
    kind = iota((locs * TAG_ONE, tokens), 0) % TAG_ONE
    for j in range(2):
        dest = loc_ref[j : j + 1]
        member = jnp.where(dest == iota((locs, tokens), 0), 1.0, 0.0)
        ahead = dot(member.astype(jnp.bfloat16), before) + base
        base += jnp.sum(member, axis=1, keepdims=True)
        rank = jnp.sum(ahead * member, axis=0, keepdims=True).astype(jnp.int32)
        select += jnp.where(dest * cap + rank == iota((locs * cap, tokens), 0), 1.0, 0.0)
        group = (group_ref[j : j + 1] + 1).astype(jnp.float32)
        row = row_ref[j : j + 1].astype(jnp.float32)
        value = jnp.where(kind == 0, group, jnp.where(kind == 1, row, 0.0))
        value = jnp.where(dest == iota((locs * TAG_ONE, tokens), 0) // TAG_ONE, value, 0.0)
        tags += dot_nt(value.astype(jnp.bfloat16), ones(rank + shift == iota((LANES, tokens), 0)))
    select = select.astype(jnp.bfloat16)
    blocks = width // LANES
    out_ref[:, blocks * cap :, :] = tags.reshape(locs, TAG_ONE, LANES).astype(jnp.bfloat16)
    read.wait()
    half = locs // PARTS
    writes = []
    for h in range(PARTS):
        dests = slice(h * half, (h + 1) * half)
        chosen = select[h * half * cap : (h + 1) * half * cap]
        for c in range(0, blocks, 2):
            part = dot(chosen, grads_ref[:, c * LANES : (c + 2) * LANES]).astype(jnp.bfloat16)
            for i in range(2):
                piece = part[:, i * LANES : (i + 1) * LANES].reshape(half, cap, LANES)
                out_ref[dests, (c + i) * cap : (c + i + 1) * cap, :] = piece
        at = pl.ds(h * half, half)
        writes.append(pltpu.make_async_copy(out_ref.at[at], to_ref.at[at], sem.at[1 + h]))
        writes[-1].start()
    for write in writes:
        write.wait()


def combine_kernel(groups, rows, cap, me_ref, came_ref, out_ref):
    locs = came_ref.shape[0]
    blocks = (came_ref.shape[1] - TAG_ONE) // cap
    lines = locs * cap // LANES
    each = locs // lines
    slots = groups * SLOTS
    tags = came_ref[:, blocks * cap :, :].astype(jnp.float32).reshape(locs * TAG_ONE, LANES)
    shape = (2 * lines, locs * TAG_ONE)
    source, kind = iota(shape, 1) // TAG_ONE, iota(shape, 1) % TAG_ONE
    pick = ones((source // each == iota(shape, 0) % lines) & (kind == iota(shape, 0) // lines))
    tags = dot(pick, tags.astype(jnp.bfloat16)).astype(jnp.int32)
    group, row = tags[:lines] - 1, tags[lines:]
    present = jnp.zeros((groups, rows), jnp.float32)
    for q in range(lines):
        in_group = ones(group[q : q + 1] == iota((groups, LANES), 0))
        in_row = ones(row[q : q + 1] == iota((rows, LANES), 0))
        present += dot_nt(in_group, in_row)
    below = ones(iota((rows, rows), 0) < iota((rows, rows), 1))
    spread = ones(iota((slots, groups), 0) // SLOTS == iota((slots, groups), 1))
    hits = dot(spread, ones(present > 0.5))
    rank = dot(hits.astype(jnp.bfloat16), below).astype(jnp.int32)
    mine = (hits > 0.5) & (rank == iota((slots, rows), 0) % SLOTS)
    slot_row = jnp.max(jnp.where(mine, iota((slots, rows), 1), -1), axis=1, keepdims=True)
    code = jnp.where(slot_row >= 0, iota((slots, 1), 0) // SLOTS * rows + slot_row, -1)
    select = jnp.concatenate(
        [ones(group[q : q + 1] * rows + row[q : q + 1] == code) for q in range(lines)], axis=1
    )
    lane = iota((slots, LANES), 1)
    mark = (lane // 16 == me_ref[0] // 2 % 8) & (lane % SLOTS == iota((slots, LANES), 0) % SLOTS)
    mark = jnp.where(mark, (slot_row + 1).astype(jnp.float32), 0.0)
    top = iota((slots, LANES), 0) % TILE < SLOTS
    pairs = groups // 2
    sums = {blocks: mark}
    tiles = {}

    def tile(low, high):
        return jnp.where(top, low, high).reshape(pairs, TILE, LANES)

    def up(x):
        return pltpu.roll(x, slots - SLOTS, 0)

    def store(t):
        both = jnp.concatenate([tiles.pop(t), tiles.pop(t + 1)], axis=1)
        out_ref[:, t * TILE : (t + 2) * TILE, :] = both.astype(jnp.bfloat16)

    for c in range(0, blocks, 2):
        part = jnp.concatenate(
            [came_ref[:, i * cap : (i + 1) * cap, :].reshape(locs * cap, LANES) for i in (c, c + 1)], axis=1
        )
        part = dot(select, part)
        sums[c], sums[c + 1] = part[:, :LANES], part[:, LANES:]
        tiles[c // 2] = tile(sums[c], pltpu.roll(sums[c + 1], SLOTS, 0))
        tiles[blocks // 2 + c // 2] = tile(up(sums[c - 1]), sums[c]) if c else tile(mark, sums[0])
        if c % 4 == 2:
            store(c // 2 - 1)
            store(blocks // 2 + c // 2 - 1)
    out_ref[:, blocks * TILE :, :] = tile(up(sums[blocks - 1]), mark).astype(jnp.bfloat16)


def update_kernel(landed_ref, table_ref, first_ref, second_ref, t_out, f_out, s_out):
    pairs = landed_ref.shape[0]
    rows, width = table_ref.shape
    blocks = width // LANES
    lines = pairs // 8
    shape = (lines, pairs * TILE)
    source, line = iota(shape, 1) // TILE // 8, iota(shape, 0)
    target = iota((4 * rows, LANES), 0) % rows
    same_block = iota((4 * rows, LANES), 0) // rows == iota((4 * rows, LANES), 1) % 16 // SLOTS
    members = []
    for at, last in ((blocks // 2 * TILE, False), (blocks * TILE, True)):
        tags = landed_ref[:, at : at + TILE, :].astype(jnp.float32).reshape(pairs * TILE, LANES)
        low = iota(shape, 1) % TILE < SLOTS
        pick = ones((source == line) & (jnp.logical_not(low) if last else low))
        tags = dot(pick, tags.astype(jnp.bfloat16)).astype(jnp.int32) - 1
        members.append(
            jnp.concatenate([ones((tags[i : i + 1] == target) & same_block) for i in range(lines)], axis=1)
        )
    found = members[0][:rows].astype(jnp.float32) + members[1][:rows].astype(jnp.float32)
    touched = jnp.max(found, axis=1, keepdims=True) > 0.5
    halves = []
    for t in range(0, blocks, 4):
        part = [
            landed_ref[:, i * TILE : (i + 2) * TILE, :].reshape(pairs * 2 * TILE, LANES) for i in (t, t + 2)
        ]
        part = dot(members[t >= blocks // 2], jnp.concatenate(part, axis=1))
        for i in range(8):
            halves.append(part[i % 4 * rows : (i % 4 + 1) * rows, i // 4 * LANES : (i // 4 + 1) * LANES])
    end = landed_ref[:, blocks * TILE :, :].astype(jnp.float32)
    end = jnp.concatenate([end, jnp.zeros_like(end)], axis=1).reshape(pairs * 2 * TILE, LANES)
    halves.append(dot(members[1][:rows], end.astype(jnp.bfloat16)))
    corr_one = 1.0 - beta_one**ADAM_STEP
    corr_two = 1.0 - beta_two**ADAM_STEP
    for c in range(blocks):
        grad = halves[c] + halves[blocks + 1 + c]
        at = slice(c * LANES, (c + 1) * LANES)
        first, second, table = first_ref[:, at], second_ref[:, at], table_ref[:, at]
        first_next = beta_one * first + (1.0 - beta_one) * grad
        second_next = beta_two * second + (1.0 - beta_two) * grad * grad
        update = learn_rate * (first_next / corr_one) / (jnp.sqrt(second_next / corr_two) + epsilon)
        t_out[:, at] = jnp.where(touched, table - update, table)
        f_out[:, at] = jnp.where(touched, first_next, first)
        s_out[:, at] = jnp.where(touched, second_next, second)


PARAMS = pltpu.CompilerParams(vmem_limit_bytes=32 << 20)
WIDE = pltpu.CompilerParams(vmem_limit_bytes=60 << 20)


def pack(me, dest, group, row, grads, locs, cap):
    width = grads.shape[1]
    shape = (locs, width // LANES * cap + TAG_ONE, LANES)
    return pl.pallas_call(
        functools.partial(pack_kernel, locs, cap),
        out_shape=jax.ShapeDtypeStruct(shape, jnp.bfloat16),
        in_specs=[SMEM, VMEM, VMEM, VMEM, ANY],
        out_specs=ANY,
        scratch_shapes=[
            pltpu.VMEM(grads.shape, jnp.bfloat16),
            pltpu.VMEM(shape, jnp.bfloat16),
            pltpu.SemaphoreType.DMA((1 + PARTS,)),
        ],
        compiler_params=WIDE,
    )(me, dest, group, row, grads)


def combine(me, came, groups, rows, cap):
    blocks = (came.shape[1] - TAG_ONE) // cap
    shape = (groups // 2, (blocks + 1) * TILE, LANES)
    return pl.pallas_call(
        functools.partial(combine_kernel, groups, rows, cap),
        out_shape=jax.ShapeDtypeStruct(shape, jnp.bfloat16),
        in_specs=[SMEM, VMEM],
        out_specs=VMEM,
        compiler_params=PARAMS,
    )(me, came)


def update(landed, table, first, second):
    return pl.pallas_call(
        update_kernel,
        out_shape=(jax.ShapeDtypeStruct(table.shape, table.dtype),) * 3,
        in_specs=[VMEM] * 4,
        out_specs=(VMEM,) * 3,
        compiler_params=PARAMS,
    )(landed, table, first, second)


def per_device(
    token_grads, owner_loc, owner_group, owner_row, embed_table, first_moment, second_moment
):
    locs = lax.axis_size("loc")
    groups = lax.axis_size("grp")
    rows = embed_table.shape[0]
    cap = 4 * token_grads.shape[0] // locs
    at_loc = lax.axis_index("loc").astype(jnp.int32).reshape(1)
    at_group = lax.axis_index("grp").astype(jnp.int32).reshape(1)
    packed = pack(at_loc, owner_loc.T, owner_group.T, owner_row.T, token_grads, locs, cap)
    came = lax.all_to_all(packed, "loc", split_axis=0, concat_axis=0, tiled=True)
    sums = combine(at_group, came, groups, rows, cap)
    shape = sums.shape
    sums = sums.reshape(groups, shape[1] // TILE, SLOTS, LANES)
    landed = lax.all_to_all(sums, "grp", split_axis=0, concat_axis=0, tiled=True).reshape(shape)
    return tuple(update(landed, embed_table, first_moment, second_moment))


def solution(mesh):
    rows = P(("grp", "loc"), None)
    return jax.shard_map(
        per_device, mesh=mesh, in_specs=(rows,) * 7, out_specs=(rows,) * 3, check_vma=False
    )
```

```python
import functools
import math

import jax
import jax.numpy as jnp
from jax import lax
from jax.experimental import pallas as pl
from jax.experimental.pallas import tpu as pltpu
from jax.sharding import PartitionSpec as P

ADAM_STEP = 100
LANES = 128
SLOTS = 4
TAG_ONE = 8
PARTS = 4
TILE = 8

beta_one = 0.9
beta_two = 0.999
learn_rate = 0.01
epsilon = 1e-08

VMEM = pl.BlockSpec(memory_space=pltpu.VMEM)
SMEM = pl.BlockSpec(memory_space=pltpu.SMEM)
ANY = pl.BlockSpec(memory_space=pl.ANY)
NT = (((1,), (1,)), ((), ()))


def iota(shape, dim):
    return lax.broadcasted_iota(jnp.int32, shape, dim)


def ones(mask):
    return jnp.where(mask, 1.0, 0.0).astype(jnp.bfloat16)


def dot(a, b):
    return jnp.dot(a, b, preferred_element_type=jnp.float32)


def dot_nt(a, b):
    return lax.dot_general(a, b, NT, preferred_element_type=jnp.float32)


def place_of(group, side):
    return group // side * 3 % side * side + group % side * 3 % side


def pack_kernel(locs, cap, side, me_ref, loc_ref, group_ref, row_ref, from_ref, to_ref, grads_ref, out_ref, sem):
    tokens, width = grads_ref.shape
    read = pltpu.make_async_copy(from_ref, grads_ref, sem.at[0])
    read.start()
    shift = me_ref[0] % (LANES // cap) * cap
    before = ones(iota((tokens, tokens), 0) < iota((tokens, tokens), 1))
    base = jnp.zeros((locs, 1), jnp.float32)
    select = jnp.zeros((locs * cap, tokens), jnp.float32)
    tags = jnp.zeros((locs * TAG_ONE, LANES), jnp.float32)
    kind = iota((locs * TAG_ONE, tokens), 0) % TAG_ONE
    for j in range(2):
        dest = loc_ref[j : j + 1]
        member = jnp.where(dest == iota((locs, tokens), 0), 1.0, 0.0)
        ahead = dot(member.astype(jnp.bfloat16), before) + base
        base += jnp.sum(member, axis=1, keepdims=True)
        rank = jnp.sum(ahead * member, axis=0, keepdims=True).astype(jnp.int32)
        select += jnp.where(dest * cap + rank == iota((locs * cap, tokens), 0), 1.0, 0.0)
        group = (place_of(group_ref[j : j + 1], side) + 1).astype(jnp.float32)
        row = row_ref[j : j + 1].astype(jnp.float32)
        value = jnp.where(kind == 0, group, jnp.where(kind == 1, row, 0.0))
        value = jnp.where(dest == iota((locs * TAG_ONE, tokens), 0) // TAG_ONE, value, 0.0)
        tags += dot_nt(value.astype(jnp.bfloat16), ones(rank + shift == iota((LANES, tokens), 0)))
    select = select.astype(jnp.bfloat16)
    blocks = width // LANES
    out_ref[:, blocks * cap :, :] = tags.reshape(locs, TAG_ONE, LANES).astype(jnp.bfloat16)
    read.wait()
    half = locs // PARTS
    writes = []
    for h in range(PARTS):
        dests = slice(h * half, (h + 1) * half)
        chosen = select[h * half * cap : (h + 1) * half * cap]
        for c in range(0, blocks, 2):
            part = dot(chosen, grads_ref[:, c * LANES : (c + 2) * LANES]).astype(jnp.bfloat16)
            for i in range(2):
                piece = part[:, i * LANES : (i + 1) * LANES].reshape(half, cap, LANES)
                out_ref[dests, (c + i) * cap : (c + i + 1) * cap, :] = piece
        at = pl.ds(h * half, half)
        writes.append(pltpu.make_async_copy(out_ref.at[at], to_ref.at[at], sem.at[1 + h]))
        writes[-1].start()
    for write in writes:
        write.wait()


def combine_kernel(groups, rows, cap, me_ref, came_ref, out_ref):
    locs = came_ref.shape[0]
    blocks = (came_ref.shape[1] - TAG_ONE) // cap
    lines = locs * cap // LANES
    each = locs // lines
    slots = groups * SLOTS
    tags = came_ref[:, blocks * cap :, :].astype(jnp.float32).reshape(locs * TAG_ONE, LANES)
    shape = (2 * lines, locs * TAG_ONE)
    source, kind = iota(shape, 1) // TAG_ONE, iota(shape, 1) % TAG_ONE
    pick = ones((source // each == iota(shape, 0) % lines) & (kind == iota(shape, 0) // lines))
    tags = dot(pick, tags.astype(jnp.bfloat16)).astype(jnp.int32)
    group, row = tags[:lines] - 1, tags[lines:]
    present = jnp.zeros((groups, rows), jnp.float32)
    for q in range(lines):
        in_group = ones(group[q : q + 1] == iota((groups, LANES), 0))
        in_row = ones(row[q : q + 1] == iota((rows, LANES), 0))
        present += dot_nt(in_group, in_row)
    below = ones(iota((rows, rows), 0) < iota((rows, rows), 1))
    spread = ones(iota((slots, groups), 0) // SLOTS == iota((slots, groups), 1))
    hits = dot(spread, ones(present > 0.5))
    rank = dot(hits.astype(jnp.bfloat16), below).astype(jnp.int32)
    mine = (hits > 0.5) & (rank == iota((slots, rows), 0) % SLOTS)
    slot_row = jnp.max(jnp.where(mine, iota((slots, rows), 1), -1), axis=1, keepdims=True)
    code = jnp.where(slot_row >= 0, iota((slots, 1), 0) // SLOTS * rows + slot_row, -1)
    select = jnp.concatenate(
        [ones(group[q : q + 1] * rows + row[q : q + 1] == code) for q in range(lines)], axis=1
    )
    lane = iota((slots, LANES), 1)
    mark = (lane // 16 == me_ref[0] // 2 % 8) & (lane % SLOTS == iota((slots, LANES), 0) % SLOTS)
    mark = jnp.where(mark, (slot_row + 1).astype(jnp.float32), 0.0)
    top = iota((slots, LANES), 0) % TILE < SLOTS
    pairs = groups // 2
    sums = {blocks: mark}
    tiles = {}

    def tile(low, high):
        return jnp.where(top, low, high).reshape(pairs, TILE, LANES)

    def up(x):
        return pltpu.roll(x, slots - SLOTS, 0)

    def store(t):
        both = jnp.concatenate([tiles.pop(t), tiles.pop(t + 1)], axis=1)
        out_ref[:, t * TILE : (t + 2) * TILE, :] = both.astype(jnp.bfloat16)

    for c in range(0, blocks, 2):
        part = jnp.concatenate(
            [came_ref[:, i * cap : (i + 1) * cap, :].reshape(locs * cap, LANES) for i in (c, c + 1)], axis=1
        )
        part = dot(select, part)
        sums[c], sums[c + 1] = part[:, :LANES], part[:, LANES:]
        tiles[c // 2] = tile(sums[c], pltpu.roll(sums[c + 1], SLOTS, 0))
        tiles[blocks // 2 + c // 2] = tile(up(sums[c - 1]), sums[c]) if c else tile(mark, sums[0])
        if c % 4 == 2:
            store(c // 2 - 1)
            store(blocks // 2 + c // 2 - 1)
    out_ref[:, blocks * TILE :, :] = tile(up(sums[blocks - 1]), mark).astype(jnp.bfloat16)


def update_kernel(landed_ref, table_ref, first_ref, second_ref, t_out, f_out, s_out):
    pairs = landed_ref.shape[0]
    rows, width = table_ref.shape
    blocks = width // LANES
    lines = pairs // 8
    shape = (lines, pairs * TILE)
    source, line = iota(shape, 1) // TILE // 8, iota(shape, 0)
    target = iota((4 * rows, LANES), 0) % rows
    same_block = iota((4 * rows, LANES), 0) // rows == iota((4 * rows, LANES), 1) % 16 // SLOTS
    members = []
    for at, last in ((blocks // 2 * TILE, False), (blocks * TILE, True)):
        tags = landed_ref[:, at : at + TILE, :].astype(jnp.float32).reshape(pairs * TILE, LANES)
        low = iota(shape, 1) % TILE < SLOTS
        pick = ones((source == line) & (jnp.logical_not(low) if last else low))
        tags = dot(pick, tags.astype(jnp.bfloat16)).astype(jnp.int32) - 1
        members.append(
            jnp.concatenate([ones((tags[i : i + 1] == target) & same_block) for i in range(lines)], axis=1)
        )
    found = members[0][:rows].astype(jnp.float32) + members[1][:rows].astype(jnp.float32)
    touched = jnp.max(found, axis=1, keepdims=True) > 0.5
    halves = []
    for t in range(0, blocks, 4):
        part = [
            landed_ref[:, i * TILE : (i + 2) * TILE, :].reshape(pairs * 2 * TILE, LANES) for i in (t, t + 2)
        ]
        part = dot(members[t >= blocks // 2], jnp.concatenate(part, axis=1))
        for i in range(8):
            halves.append(part[i % 4 * rows : (i % 4 + 1) * rows, i // 4 * LANES : (i // 4 + 1) * LANES])
    end = landed_ref[:, blocks * TILE :, :].astype(jnp.float32)
    end = jnp.concatenate([end, jnp.zeros_like(end)], axis=1).reshape(pairs * 2 * TILE, LANES)
    halves.append(dot(members[1][:rows], end.astype(jnp.bfloat16)))
    corr_one = 1.0 - beta_one**ADAM_STEP
    corr_two = 1.0 - beta_two**ADAM_STEP
    for c in range(blocks):
        grad = halves[c] + halves[blocks + 1 + c]
        at = slice(c * LANES, (c + 1) * LANES)
        first, second, table = first_ref[:, at], second_ref[:, at], table_ref[:, at]
        first_next = beta_one * first + (1.0 - beta_one) * grad
        second_next = beta_two * second + (1.0 - beta_two) * grad * grad
        update = learn_rate * (first_next / corr_one) / (jnp.sqrt(second_next / corr_two) + epsilon)
        t_out[:, at] = jnp.where(touched, table - update, table)
        f_out[:, at] = jnp.where(touched, first_next, first)
        s_out[:, at] = jnp.where(touched, second_next, second)


PARAMS = pltpu.CompilerParams(vmem_limit_bytes=32 << 20)
WIDE = pltpu.CompilerParams(vmem_limit_bytes=60 << 20)


def pack(me, dest, group, row, grads, locs, cap, side):
    width = grads.shape[1]
    shape = (locs, width // LANES * cap + TAG_ONE, LANES)
    return pl.pallas_call(
        functools.partial(pack_kernel, locs, cap, side),
        out_shape=jax.ShapeDtypeStruct(shape, jnp.bfloat16),
        in_specs=[SMEM, VMEM, VMEM, VMEM, ANY],
        out_specs=ANY,
        scratch_shapes=[
            pltpu.VMEM(grads.shape, jnp.bfloat16),
            pltpu.VMEM(shape, jnp.bfloat16),
            pltpu.SemaphoreType.DMA((1 + PARTS,)),
        ],
        compiler_params=WIDE,
    )(me, dest, group, row, grads)


def combine(me, came, groups, rows, cap):
    blocks = (came.shape[1] - TAG_ONE) // cap
    shape = (groups // 2, (blocks + 1) * TILE, LANES)
    return pl.pallas_call(
        functools.partial(combine_kernel, groups, rows, cap),
        out_shape=jax.ShapeDtypeStruct(shape, jnp.bfloat16),
        in_specs=[SMEM, VMEM],
        out_specs=VMEM,
        compiler_params=PARAMS,
    )(me, came)


def update(landed, table, first, second):
    return pl.pallas_call(
        update_kernel,
        out_shape=(jax.ShapeDtypeStruct(table.shape, table.dtype),) * 3,
        in_specs=[VMEM] * 4,
        out_specs=(VMEM,) * 3,
        compiler_params=PARAMS,
    )(landed, table, first, second)


def per_device(
    token_grads, owner_loc, owner_group, owner_row, embed_table, first_moment, second_moment
):
    locs = lax.axis_size("loc")
    groups = lax.axis_size("grp")
    rows = embed_table.shape[0]
    cap = 4 * token_grads.shape[0] // locs
    at_loc = lax.axis_index("loc").astype(jnp.int32).reshape(1)
    side = math.isqrt(groups)
    at_group = place_of(lax.axis_index("grp").astype(jnp.int32), side).reshape(1)
    order = [place_of(g, side) for g in range(groups)]
    packed = pack(at_loc, owner_loc.T, owner_group.T, owner_row.T, token_grads, locs, cap, side)
    came = lax.all_to_all(packed, "loc", split_axis=0, concat_axis=0, tiled=True)
    sums = combine(at_group, came, groups, rows, cap)
    shape = sums.shape
    sums = sums.reshape(groups, shape[1] // TILE, SLOTS, LANES)
    landed = lax.all_to_all(
        sums, "grp", split_axis=0, concat_axis=0, tiled=True, axis_index_groups=[order]
    ).reshape(shape)
    return tuple(update(landed, embed_table, first_moment, second_moment))


def solution(mesh):
    rows = P(("grp", "loc"), None)
    return jax.shard_map(
        per_device, mesh=mesh, in_specs=(rows,) * 7, out_specs=(rows,) * 3, check_vma=False
    )
```

```python
import functools
import math

import jax
import jax.numpy as jnp
from jax import lax
from jax.experimental import pallas as pl
from jax.experimental.pallas import tpu as pltpu
from jax.sharding import PartitionSpec as P

ADAM_STEP = 100
LANES = 128
SLOTS = 4
TAG_ONE = 8
PARTS = 4
TILE = 8

beta_one = 0.9
beta_two = 0.999
learn_rate = 0.01
epsilon = 1e-08

VMEM = pl.BlockSpec(memory_space=pltpu.VMEM)
SMEM = pl.BlockSpec(memory_space=pltpu.SMEM)
ANY = pl.BlockSpec(memory_space=pl.ANY)
NT = (((1,), (1,)), ((), ()))


def iota(shape, dim):
    return lax.broadcasted_iota(jnp.int32, shape, dim)


def ones(mask):
    return jnp.where(mask, 1.0, 0.0).astype(jnp.bfloat16)


def dot(a, b):
    return jnp.dot(a, b, preferred_element_type=jnp.float32)


def dot_nt(a, b):
    return lax.dot_general(a, b, NT, preferred_element_type=jnp.float32)


def group_place(group, side):
    return group % side * side + group // side


def loc_place(loc, locs):
    return loc % 2 * (locs // 2) + loc // 2


def pack_kernel(locs, cap, side, me_ref, loc_ref, group_ref, row_ref, from_ref, to_ref, grads_ref, out_ref, sem):
    tokens, width = grads_ref.shape
    read = pltpu.make_async_copy(from_ref, grads_ref, sem.at[0])
    read.start()
    shift = me_ref[0] % (LANES // cap) * cap
    before = ones(iota((tokens, tokens), 0) < iota((tokens, tokens), 1))
    base = jnp.zeros((locs, 1), jnp.float32)
    select = jnp.zeros((locs * cap, tokens), jnp.float32)
    tags = jnp.zeros((locs * TAG_ONE, LANES), jnp.float32)
    kind = iota((locs * TAG_ONE, tokens), 0) % TAG_ONE
    for j in range(2):
        dest = loc_place(loc_ref[j : j + 1], locs)
        member = jnp.where(dest == iota((locs, tokens), 0), 1.0, 0.0)
        ahead = dot(member.astype(jnp.bfloat16), before) + base
        base += jnp.sum(member, axis=1, keepdims=True)
        rank = jnp.sum(ahead * member, axis=0, keepdims=True).astype(jnp.int32)
        select += jnp.where(dest * cap + rank == iota((locs * cap, tokens), 0), 1.0, 0.0)
        group = (group_place(group_ref[j : j + 1], side) + 1).astype(jnp.float32)
        row = row_ref[j : j + 1].astype(jnp.float32)
        value = jnp.where(kind == 0, group, jnp.where(kind == 1, row, 0.0))
        value = jnp.where(dest == iota((locs * TAG_ONE, tokens), 0) // TAG_ONE, value, 0.0)
        tags += dot_nt(value.astype(jnp.bfloat16), ones(rank + shift == iota((LANES, tokens), 0)))
    select = select.astype(jnp.bfloat16)
    blocks = width // LANES
    out_ref[:, blocks * cap :, :] = tags.reshape(locs, TAG_ONE, LANES).astype(jnp.bfloat16)
    read.wait()
    half = locs // PARTS
    writes = []
    for h in range(PARTS):
        dests = slice(h * half, (h + 1) * half)
        chosen = select[h * half * cap : (h + 1) * half * cap]
        for c in range(0, blocks, 2):
            part = dot(chosen, grads_ref[:, c * LANES : (c + 2) * LANES]).astype(jnp.bfloat16)
            for i in range(2):
                piece = part[:, i * LANES : (i + 1) * LANES].reshape(half, cap, LANES)
                out_ref[dests, (c + i) * cap : (c + i + 1) * cap, :] = piece
        at = pl.ds(h * half, half)
        writes.append(pltpu.make_async_copy(out_ref.at[at], to_ref.at[at], sem.at[1 + h]))
        writes[-1].start()
    for write in writes:
        write.wait()


def combine_kernel(groups, rows, cap, me_ref, came_ref, out_ref):
    locs = came_ref.shape[0]
    blocks = (came_ref.shape[1] - TAG_ONE) // cap
    lines = locs * cap // LANES
    each = locs // lines
    slots = groups * SLOTS
    tags = came_ref[:, blocks * cap :, :].astype(jnp.float32).reshape(locs * TAG_ONE, LANES)
    shape = (2 * lines, locs * TAG_ONE)
    source, kind = iota(shape, 1) // TAG_ONE, iota(shape, 1) % TAG_ONE
    pick = ones((source // each == iota(shape, 0) % lines) & (kind == iota(shape, 0) // lines))
    tags = dot(pick, tags.astype(jnp.bfloat16)).astype(jnp.int32)
    group, row = tags[:lines] - 1, tags[lines:]
    present = jnp.zeros((groups, rows), jnp.float32)
    for q in range(lines):
        in_group = ones(group[q : q + 1] == iota((groups, LANES), 0))
        in_row = ones(row[q : q + 1] == iota((rows, LANES), 0))
        present += dot_nt(in_group, in_row)
    below = ones(iota((rows, rows), 0) < iota((rows, rows), 1))
    spread = ones(iota((slots, groups), 0) // SLOTS == iota((slots, groups), 1))
    hits = dot(spread, ones(present > 0.5))
    rank = dot(hits.astype(jnp.bfloat16), below).astype(jnp.int32)
    mine = (hits > 0.5) & (rank == iota((slots, rows), 0) % SLOTS)
    slot_row = jnp.max(jnp.where(mine, iota((slots, rows), 1), -1), axis=1, keepdims=True)
    code = jnp.where(slot_row >= 0, iota((slots, 1), 0) // SLOTS * rows + slot_row, -1)
    select = jnp.concatenate(
        [ones(group[q : q + 1] * rows + row[q : q + 1] == code) for q in range(lines)], axis=1
    )
    lane = iota((slots, LANES), 1)
    mark = (lane // 16 == me_ref[0] // 2 % 8) & (lane % SLOTS == iota((slots, LANES), 0) % SLOTS)
    mark = jnp.where(mark, (slot_row + 1).astype(jnp.float32), 0.0)
    top = iota((slots, LANES), 0) % TILE < SLOTS
    pairs = groups // 2
    sums = {blocks: mark}
    tiles = {}

    def tile(low, high):
        return jnp.where(top, low, high).reshape(pairs, TILE, LANES)

    def up(x):
        return pltpu.roll(x, slots - SLOTS, 0)

    def store(t):
        both = jnp.concatenate([tiles.pop(t), tiles.pop(t + 1)], axis=1)
        out_ref[:, t * TILE : (t + 2) * TILE, :] = both.astype(jnp.bfloat16)

    for c in range(0, blocks, 2):
        part = jnp.concatenate(
            [came_ref[:, i * cap : (i + 1) * cap, :].reshape(locs * cap, LANES) for i in (c, c + 1)], axis=1
        )
        part = dot(select, part)
        sums[c], sums[c + 1] = part[:, :LANES], part[:, LANES:]
        tiles[c // 2] = tile(sums[c], pltpu.roll(sums[c + 1], SLOTS, 0))
        tiles[blocks // 2 + c // 2] = tile(up(sums[c - 1]), sums[c]) if c else tile(mark, sums[0])
        if c % 4 == 2:
            store(c // 2 - 1)
            store(blocks // 2 + c // 2 - 1)
    out_ref[:, blocks * TILE :, :] = tile(up(sums[blocks - 1]), mark).astype(jnp.bfloat16)


def update_kernel(landed_ref, table_ref, first_ref, second_ref, t_out, f_out, s_out):
    pairs = landed_ref.shape[0]
    rows, width = table_ref.shape
    blocks = width // LANES
    lines = pairs // 8
    shape = (lines, pairs * TILE)
    source, line = iota(shape, 1) // TILE // 8, iota(shape, 0)
    target = iota((4 * rows, LANES), 0) % rows
    same_block = iota((4 * rows, LANES), 0) // rows == iota((4 * rows, LANES), 1) % 16 // SLOTS
    members = []
    for at, last in ((blocks // 2 * TILE, False), (blocks * TILE, True)):
        tags = landed_ref[:, at : at + TILE, :].astype(jnp.float32).reshape(pairs * TILE, LANES)
        low = iota(shape, 1) % TILE < SLOTS
        pick = ones((source == line) & (jnp.logical_not(low) if last else low))
        tags = dot(pick, tags.astype(jnp.bfloat16)).astype(jnp.int32) - 1
        members.append(
            jnp.concatenate([ones((tags[i : i + 1] == target) & same_block) for i in range(lines)], axis=1)
        )
    found = members[0][:rows].astype(jnp.float32) + members[1][:rows].astype(jnp.float32)
    touched = jnp.max(found, axis=1, keepdims=True) > 0.5
    halves = []
    for t in range(0, blocks, 4):
        part = [
            landed_ref[:, i * TILE : (i + 2) * TILE, :].reshape(pairs * 2 * TILE, LANES) for i in (t, t + 2)
        ]
        part = dot(members[t >= blocks // 2], jnp.concatenate(part, axis=1))
        for i in range(8):
            halves.append(part[i % 4 * rows : (i % 4 + 1) * rows, i // 4 * LANES : (i // 4 + 1) * LANES])
    end = landed_ref[:, blocks * TILE :, :].astype(jnp.float32)
    end = jnp.concatenate([end, jnp.zeros_like(end)], axis=1).reshape(pairs * 2 * TILE, LANES)
    halves.append(dot(members[1][:rows], end.astype(jnp.bfloat16)))
    corr_one = 1.0 - beta_one**ADAM_STEP
    corr_two = 1.0 - beta_two**ADAM_STEP
    for c in range(blocks):
        grad = halves[c] + halves[blocks + 1 + c]
        at = slice(c * LANES, (c + 1) * LANES)
        first, second, table = first_ref[:, at], second_ref[:, at], table_ref[:, at]
        first_next = beta_one * first + (1.0 - beta_one) * grad
        second_next = beta_two * second + (1.0 - beta_two) * grad * grad
        update = learn_rate * (first_next / corr_one) / (jnp.sqrt(second_next / corr_two) + epsilon)
        t_out[:, at] = jnp.where(touched, table - update, table)
        f_out[:, at] = jnp.where(touched, first_next, first)
        s_out[:, at] = jnp.where(touched, second_next, second)


PARAMS = pltpu.CompilerParams(vmem_limit_bytes=32 << 20)
WIDE = pltpu.CompilerParams(vmem_limit_bytes=60 << 20)


def pack(me, dest, group, row, grads, locs, cap, side):
    width = grads.shape[1]
    shape = (locs, width // LANES * cap + TAG_ONE, LANES)
    return pl.pallas_call(
        functools.partial(pack_kernel, locs, cap, side),
        out_shape=jax.ShapeDtypeStruct(shape, jnp.bfloat16),
        in_specs=[SMEM, VMEM, VMEM, VMEM, ANY],
        out_specs=ANY,
        scratch_shapes=[
            pltpu.VMEM(grads.shape, jnp.bfloat16),
            pltpu.VMEM(shape, jnp.bfloat16),
            pltpu.SemaphoreType.DMA((1 + PARTS,)),
        ],
        compiler_params=WIDE,
    )(me, dest, group, row, grads)


def combine(me, came, groups, rows, cap):
    blocks = (came.shape[1] - TAG_ONE) // cap
    shape = (groups // 2, (blocks + 1) * TILE, LANES)
    return pl.pallas_call(
        functools.partial(combine_kernel, groups, rows, cap),
        out_shape=jax.ShapeDtypeStruct(shape, jnp.bfloat16),
        in_specs=[SMEM, VMEM],
        out_specs=VMEM,
        compiler_params=PARAMS,
    )(me, came)


def update(landed, table, first, second):
    return pl.pallas_call(
        update_kernel,
        out_shape=(jax.ShapeDtypeStruct(table.shape, table.dtype),) * 3,
        in_specs=[VMEM] * 4,
        out_specs=(VMEM,) * 3,
        compiler_params=PARAMS,
    )(landed, table, first, second)


def per_device(
    token_grads, owner_loc, owner_group, owner_row, embed_table, first_moment, second_moment
):
    locs = lax.axis_size("loc")
    groups = lax.axis_size("grp")
    rows = embed_table.shape[0]
    cap = 4 * token_grads.shape[0] // locs
    at_loc = loc_place(lax.axis_index("loc").astype(jnp.int32), locs).reshape(1)
    loc_order = sorted(range(locs), key=lambda loc: loc_place(loc, locs))
    side = math.isqrt(groups)
    at_group = group_place(lax.axis_index("grp").astype(jnp.int32), side).reshape(1)
    group_order = [group_place(g, side) for g in range(groups)]
    packed = pack(at_loc, owner_loc.T, owner_group.T, owner_row.T, token_grads, locs, cap, side)
    came = lax.all_to_all(
        packed, "loc", split_axis=0, concat_axis=0, tiled=True, axis_index_groups=[loc_order]
    )
    sums = combine(at_group, came, groups, rows, cap)
    shape = sums.shape
    sums = sums.reshape(groups, shape[1] // TILE, SLOTS, LANES)
    landed = lax.all_to_all(
        sums, "grp", split_axis=0, concat_axis=0, tiled=True, axis_index_groups=[group_order]
    ).reshape(shape)
    return tuple(update(landed, embed_table, first_moment, second_moment))


def solution(mesh):
    rows = P(("grp", "loc"), None)
    return jax.shard_map(
        per_device, mesh=mesh, in_specs=(rows,) * 7, out_specs=(rows,) * 3, check_vma=False
    )
```

```python
import functools
import math

import jax
import jax.numpy as jnp
from jax import lax
from jax.experimental import pallas as pl
from jax.experimental.pallas import tpu as pltpu
from jax.sharding import PartitionSpec as P

ADAM_STEP = 100
LANES = 128
SLOTS = 4
TAG_ONE = 8
PARTS = 4
TILE = 8

beta_one = 0.9
beta_two = 0.999
learn_rate = 0.01
epsilon = 1e-08

VMEM = pl.BlockSpec(memory_space=pltpu.VMEM)
SMEM = pl.BlockSpec(memory_space=pltpu.SMEM)
ANY = pl.BlockSpec(memory_space=pl.ANY)
NT = (((1,), (1,)), ((), ()))


def iota(shape, dim):
    return lax.broadcasted_iota(jnp.int32, shape, dim)


def ones(mask):
    return jnp.where(mask, 1.0, 0.0).astype(jnp.bfloat16)


def dot(a, b):
    return jnp.dot(a, b, preferred_element_type=jnp.float32)


def dot_nt(a, b):
    return lax.dot_general(a, b, NT, preferred_element_type=jnp.float32)


def group_place(group, side):
    return (group // side - group % side + side) % side * side + group % side


def loc_place(loc, locs):
    return loc % 2 * (locs // 2) + loc // 2


def pack_kernel(locs, cap, side, me_ref, loc_ref, group_ref, row_ref, from_ref, to_ref, grads_ref, out_ref, sem):
    tokens, width = grads_ref.shape
    read = pltpu.make_async_copy(from_ref, grads_ref, sem.at[0])
    read.start()
    shift = me_ref[0] % (LANES // cap) * cap
    before = ones(iota((tokens, tokens), 0) < iota((tokens, tokens), 1))
    base = jnp.zeros((locs, 1), jnp.float32)
    select = jnp.zeros((locs * cap, tokens), jnp.float32)
    tags = jnp.zeros((locs * TAG_ONE, LANES), jnp.float32)
    kind = iota((locs * TAG_ONE, tokens), 0) % TAG_ONE
    for j in range(2):
        dest = loc_place(loc_ref[j : j + 1], locs)
        member = jnp.where(dest == iota((locs, tokens), 0), 1.0, 0.0)
        ahead = dot(member.astype(jnp.bfloat16), before) + base
        base += jnp.sum(member, axis=1, keepdims=True)
        rank = jnp.sum(ahead * member, axis=0, keepdims=True).astype(jnp.int32)
        select += jnp.where(dest * cap + rank == iota((locs * cap, tokens), 0), 1.0, 0.0)
        group = (group_place(group_ref[j : j + 1], side) + 1).astype(jnp.float32)
        row = row_ref[j : j + 1].astype(jnp.float32)
        value = jnp.where(kind == 0, group, jnp.where(kind == 1, row, 0.0))
        value = jnp.where(dest == iota((locs * TAG_ONE, tokens), 0) // TAG_ONE, value, 0.0)
        tags += dot_nt(value.astype(jnp.bfloat16), ones(rank + shift == iota((LANES, tokens), 0)))
    select = select.astype(jnp.bfloat16)
    blocks = width // LANES
    out_ref[:, blocks * cap :, :] = tags.reshape(locs, TAG_ONE, LANES).astype(jnp.bfloat16)
    read.wait()
    half = locs // PARTS
    writes = []
    for h in range(PARTS):
        dests = slice(h * half, (h + 1) * half)
        chosen = select[h * half * cap : (h + 1) * half * cap]
        for c in range(0, blocks, 2):
            part = dot(chosen, grads_ref[:, c * LANES : (c + 2) * LANES]).astype(jnp.bfloat16)
            for i in range(2):
                piece = part[:, i * LANES : (i + 1) * LANES].reshape(half, cap, LANES)
                out_ref[dests, (c + i) * cap : (c + i + 1) * cap, :] = piece
        at = pl.ds(h * half, half)
        writes.append(pltpu.make_async_copy(out_ref.at[at], to_ref.at[at], sem.at[1 + h]))
        writes[-1].start()
    for write in writes:
        write.wait()


def combine_kernel(groups, rows, cap, me_ref, came_ref, out_ref):
    locs = came_ref.shape[0]
    blocks = (came_ref.shape[1] - TAG_ONE) // cap
    lines = locs * cap // LANES
    each = locs // lines
    slots = groups * SLOTS
    tags = came_ref[:, blocks * cap :, :].astype(jnp.float32).reshape(locs * TAG_ONE, LANES)
    shape = (2 * lines, locs * TAG_ONE)
    source, kind = iota(shape, 1) // TAG_ONE, iota(shape, 1) % TAG_ONE
    pick = ones((source // each == iota(shape, 0) % lines) & (kind == iota(shape, 0) // lines))
    tags = dot(pick, tags.astype(jnp.bfloat16)).astype(jnp.int32)
    group, row = tags[:lines] - 1, tags[lines:]
    present = jnp.zeros((groups, rows), jnp.float32)
    for q in range(lines):
        in_group = ones(group[q : q + 1] == iota((groups, LANES), 0))
        in_row = ones(row[q : q + 1] == iota((rows, LANES), 0))
        present += dot_nt(in_group, in_row)
    below = ones(iota((rows, rows), 0) < iota((rows, rows), 1))
    spread = ones(iota((slots, groups), 0) // SLOTS == iota((slots, groups), 1))
    hits = dot(spread, ones(present > 0.5))
    rank = dot(hits.astype(jnp.bfloat16), below).astype(jnp.int32)
    mine = (hits > 0.5) & (rank == iota((slots, rows), 0) % SLOTS)
    slot_row = jnp.max(jnp.where(mine, iota((slots, rows), 1), -1), axis=1, keepdims=True)
    code = jnp.where(slot_row >= 0, iota((slots, 1), 0) // SLOTS * rows + slot_row, -1)
    select = jnp.concatenate(
        [ones(group[q : q + 1] * rows + row[q : q + 1] == code) for q in range(lines)], axis=1
    )
    lane = iota((slots, LANES), 1)
    mark = (lane // 16 == me_ref[0] // 2 % 8) & (lane % SLOTS == iota((slots, LANES), 0) % SLOTS)
    mark = jnp.where(mark, (slot_row + 1).astype(jnp.float32), 0.0)
    top = iota((slots, LANES), 0) % TILE < SLOTS
    pairs = groups // 2
    sums = {blocks: mark}
    tiles = {}

    def tile(low, high):
        return jnp.where(top, low, high).reshape(pairs, TILE, LANES)

    def up(x):
        return pltpu.roll(x, slots - SLOTS, 0)

    def store(t):
        both = jnp.concatenate([tiles.pop(t), tiles.pop(t + 1)], axis=1)
        out_ref[:, t * TILE : (t + 2) * TILE, :] = both.astype(jnp.bfloat16)

    for c in range(0, blocks, 2):
        part = jnp.concatenate(
            [came_ref[:, i * cap : (i + 1) * cap, :].reshape(locs * cap, LANES) for i in (c, c + 1)], axis=1
        )
        part = dot(select, part)
        sums[c], sums[c + 1] = part[:, :LANES], part[:, LANES:]
        tiles[c // 2] = tile(sums[c], pltpu.roll(sums[c + 1], SLOTS, 0))
        tiles[blocks // 2 + c // 2] = tile(up(sums[c - 1]), sums[c]) if c else tile(mark, sums[0])
        if c % 4 == 2:
            store(c // 2 - 1)
            store(blocks // 2 + c // 2 - 1)
    out_ref[:, blocks * TILE :, :] = tile(up(sums[blocks - 1]), mark).astype(jnp.bfloat16)


def update_kernel(landed_ref, table_ref, first_ref, second_ref, t_out, f_out, s_out):
    pairs = landed_ref.shape[0]
    rows, width = table_ref.shape
    blocks = width // LANES
    lines = pairs // 8
    shape = (lines, pairs * TILE)
    source, line = iota(shape, 1) // TILE // 8, iota(shape, 0)
    target = iota((4 * rows, LANES), 0) % rows
    same_block = iota((4 * rows, LANES), 0) // rows == iota((4 * rows, LANES), 1) % 16 // SLOTS
    members = []
    for at, last in ((blocks // 2 * TILE, False), (blocks * TILE, True)):
        tags = landed_ref[:, at : at + TILE, :].astype(jnp.float32).reshape(pairs * TILE, LANES)
        low = iota(shape, 1) % TILE < SLOTS
        pick = ones((source == line) & (jnp.logical_not(low) if last else low))
        tags = dot(pick, tags.astype(jnp.bfloat16)).astype(jnp.int32) - 1
        members.append(
            jnp.concatenate([ones((tags[i : i + 1] == target) & same_block) for i in range(lines)], axis=1)
        )
    found = members[0][:rows].astype(jnp.float32) + members[1][:rows].astype(jnp.float32)
    touched = jnp.max(found, axis=1, keepdims=True) > 0.5
    halves = []
    for t in range(0, blocks, 4):
        part = [
            landed_ref[:, i * TILE : (i + 2) * TILE, :].reshape(pairs * 2 * TILE, LANES) for i in (t, t + 2)
        ]
        part = dot(members[t >= blocks // 2], jnp.concatenate(part, axis=1))
        for i in range(8):
            halves.append(part[i % 4 * rows : (i % 4 + 1) * rows, i // 4 * LANES : (i // 4 + 1) * LANES])
    end = landed_ref[:, blocks * TILE :, :].astype(jnp.float32)
    end = jnp.concatenate([end, jnp.zeros_like(end)], axis=1).reshape(pairs * 2 * TILE, LANES)
    halves.append(dot(members[1][:rows], end.astype(jnp.bfloat16)))
    corr_one = 1.0 - beta_one**ADAM_STEP
    corr_two = 1.0 - beta_two**ADAM_STEP
    for c in range(blocks):
        grad = halves[c] + halves[blocks + 1 + c]
        at = slice(c * LANES, (c + 1) * LANES)
        first, second, table = first_ref[:, at], second_ref[:, at], table_ref[:, at]
        first_next = beta_one * first + (1.0 - beta_one) * grad
        second_next = beta_two * second + (1.0 - beta_two) * grad * grad
        update = learn_rate * (first_next / corr_one) / (jnp.sqrt(second_next / corr_two) + epsilon)
        t_out[:, at] = jnp.where(touched, table - update, table)
        f_out[:, at] = jnp.where(touched, first_next, first)
        s_out[:, at] = jnp.where(touched, second_next, second)


PARAMS = pltpu.CompilerParams(vmem_limit_bytes=32 << 20)
WIDE = pltpu.CompilerParams(vmem_limit_bytes=60 << 20)


def pack(me, dest, group, row, grads, locs, cap, side):
    width = grads.shape[1]
    shape = (locs, width // LANES * cap + TAG_ONE, LANES)
    return pl.pallas_call(
        functools.partial(pack_kernel, locs, cap, side),
        out_shape=jax.ShapeDtypeStruct(shape, jnp.bfloat16),
        in_specs=[SMEM, VMEM, VMEM, VMEM, ANY],
        out_specs=ANY,
        scratch_shapes=[
            pltpu.VMEM(grads.shape, jnp.bfloat16),
            pltpu.VMEM(shape, jnp.bfloat16),
            pltpu.SemaphoreType.DMA((1 + PARTS,)),
        ],
        compiler_params=WIDE,
    )(me, dest, group, row, grads)


def combine(me, came, groups, rows, cap):
    blocks = (came.shape[1] - TAG_ONE) // cap
    shape = (groups // 2, (blocks + 1) * TILE, LANES)
    return pl.pallas_call(
        functools.partial(combine_kernel, groups, rows, cap),
        out_shape=jax.ShapeDtypeStruct(shape, jnp.bfloat16),
        in_specs=[SMEM, VMEM],
        out_specs=VMEM,
        compiler_params=PARAMS,
    )(me, came)


def update(landed, table, first, second):
    return pl.pallas_call(
        update_kernel,
        out_shape=(jax.ShapeDtypeStruct(table.shape, table.dtype),) * 3,
        in_specs=[VMEM] * 4,
        out_specs=(VMEM,) * 3,
        compiler_params=PARAMS,
    )(landed, table, first, second)


def per_device(
    token_grads, owner_loc, owner_group, owner_row, embed_table, first_moment, second_moment
):
    locs = lax.axis_size("loc")
    groups = lax.axis_size("grp")
    rows = embed_table.shape[0]
    cap = 4 * token_grads.shape[0] // locs
    at_loc = loc_place(lax.axis_index("loc").astype(jnp.int32), locs).reshape(1)
    loc_order = sorted(range(locs), key=lambda loc: loc_place(loc, locs))
    side = math.isqrt(groups)
    at_group = group_place(lax.axis_index("grp").astype(jnp.int32), side).reshape(1)
    group_order = sorted(range(groups), key=lambda group: group_place(group, side))
    packed = pack(at_loc, owner_loc.T, owner_group.T, owner_row.T, token_grads, locs, cap, side)
    came = lax.all_to_all(
        packed, "loc", split_axis=0, concat_axis=0, tiled=True, axis_index_groups=[loc_order]
    )
    sums = combine(at_group, came, groups, rows, cap)
    shape = sums.shape
    sums = sums.reshape(groups, shape[1] // TILE, SLOTS, LANES)
    landed = lax.all_to_all(
        sums, "grp", split_axis=0, concat_axis=0, tiled=True, axis_index_groups=[group_order]
    ).reshape(shape)
    return tuple(update(landed, embed_table, first_moment, second_moment))


def solution(mesh):
    rows = P(("grp", "loc"), None)
    return jax.shard_map(
        per_device, mesh=mesh, in_specs=(rows,) * 7, out_specs=(rows,) * 3, check_vma=False
    )
```

```python
import functools
import math

import jax
import jax.numpy as jnp
from jax import lax
from jax.experimental import pallas as pl
from jax.experimental.pallas import tpu as pltpu
from jax.sharding import PartitionSpec as P

ADAM_STEP = 100
LANES = 128
SLOTS = 4
TAG_ONE = 8
PARTS = 4
TILE = 8

beta_one = 0.9
beta_two = 0.999
learn_rate = 0.01
epsilon = 1e-08

VMEM = pl.BlockSpec(memory_space=pltpu.VMEM)
SMEM = pl.BlockSpec(memory_space=pltpu.SMEM)
ANY = pl.BlockSpec(memory_space=pl.ANY)
NT = (((1,), (1,)), ((), ()))


def iota(shape, dim):
    return lax.broadcasted_iota(jnp.int32, shape, dim)


def ones(mask):
    return jnp.where(mask, 1.0, 0.0).astype(jnp.bfloat16)


def dot(a, b):
    return jnp.dot(a, b, preferred_element_type=jnp.float32)


def dot_nt(a, b):
    return lax.dot_general(a, b, NT, preferred_element_type=jnp.float32)


def group_place(group, side):
    return group % side * side + group // side


def loc_place(loc, locs):
    return loc % 2 * (locs // 2) + loc // 2


def pack_kernel(locs, cap, side, me_ref, loc_from, group_from, row_from, from_ref, to_ref, *scratch):
    loc_ref, group_ref, row_ref, grads_ref, out_ref, sem = scratch
    sources = (loc_from, group_from, row_from, from_ref)
    reads = [pltpu.make_async_copy(a, b, sem.at[i]) for i, (a, b) in enumerate(zip(sources, scratch))]
    for read in reads:
        read.start()
    tokens, width = grads_ref.shape
    for read in reads[:3]:
        read.wait()
    shift = me_ref[0] % (LANES // cap) * cap
    before = ones(iota((tokens, tokens), 0) < iota((tokens, tokens), 1))
    base = jnp.zeros((locs, 1), jnp.float32)
    select = jnp.zeros((locs * cap, tokens), jnp.float32)
    tags = jnp.zeros((locs * TAG_ONE, LANES), jnp.float32)
    kind = iota((locs * TAG_ONE, tokens), 0) % TAG_ONE
    for j in range(2):
        dest = loc_place(loc_ref[j : j + 1], locs)
        member = jnp.where(dest == iota((locs, tokens), 0), 1.0, 0.0)
        ahead = dot(member.astype(jnp.bfloat16), before) + base
        base += jnp.sum(member, axis=1, keepdims=True)
        rank = jnp.sum(ahead * member, axis=0, keepdims=True).astype(jnp.int32)
        select += jnp.where(dest * cap + rank == iota((locs * cap, tokens), 0), 1.0, 0.0)
        group = (group_place(group_ref[j : j + 1], side) + 1).astype(jnp.float32)
        row = row_ref[j : j + 1].astype(jnp.float32)
        value = jnp.where(kind == 0, group, jnp.where(kind == 1, row, 0.0))
        value = jnp.where(dest == iota((locs * TAG_ONE, tokens), 0) // TAG_ONE, value, 0.0)
        tags += dot_nt(value.astype(jnp.bfloat16), ones(rank + shift == iota((LANES, tokens), 0)))
    select = select.astype(jnp.bfloat16)
    blocks = width // LANES
    out_ref[:, blocks * cap :, :] = tags.reshape(locs, TAG_ONE, LANES).astype(jnp.bfloat16)
    reads[3].wait()
    half = locs // PARTS
    writes = []
    for h in range(PARTS):
        dests = slice(h * half, (h + 1) * half)
        chosen = select[h * half * cap : (h + 1) * half * cap]
        for c in range(0, blocks, 2):
            part = dot(chosen, grads_ref[:, c * LANES : (c + 2) * LANES]).astype(jnp.bfloat16)
            for i in range(2):
                piece = part[:, i * LANES : (i + 1) * LANES].reshape(half, cap, LANES)
                out_ref[dests, (c + i) * cap : (c + i + 1) * cap, :] = piece
        at = pl.ds(h * half, half)
        writes.append(pltpu.make_async_copy(out_ref.at[at], to_ref.at[at], sem.at[len(reads) + h]))
        writes[-1].start()
    for write in writes:
        write.wait()


def combine_kernel(groups, rows, cap, me_ref, came_ref, out_ref):
    locs = came_ref.shape[0]
    blocks = (came_ref.shape[1] - TAG_ONE) // cap
    lines = locs * cap // LANES
    each = locs // lines
    slots = groups * SLOTS
    tags = came_ref[:, blocks * cap :, :].astype(jnp.float32).reshape(locs * TAG_ONE, LANES)
    shape = (2 * lines, locs * TAG_ONE)
    source, kind = iota(shape, 1) // TAG_ONE, iota(shape, 1) % TAG_ONE
    pick = ones((source // each == iota(shape, 0) % lines) & (kind == iota(shape, 0) // lines))
    tags = dot(pick, tags.astype(jnp.bfloat16)).astype(jnp.int32)
    group, row = tags[:lines] - 1, tags[lines:]
    present = jnp.zeros((groups, rows), jnp.float32)
    for q in range(lines):
        in_group = ones(group[q : q + 1] == iota((groups, LANES), 0))
        in_row = ones(row[q : q + 1] == iota((rows, LANES), 0))
        present += dot_nt(in_group, in_row)
    below = ones(iota((rows, rows), 0) < iota((rows, rows), 1))
    spread = ones(iota((slots, groups), 0) // SLOTS == iota((slots, groups), 1))
    hits = dot(spread, ones(present > 0.5))
    rank = dot(hits.astype(jnp.bfloat16), below).astype(jnp.int32)
    mine = (hits > 0.5) & (rank == iota((slots, rows), 0) % SLOTS)
    slot_row = jnp.max(jnp.where(mine, iota((slots, rows), 1), -1), axis=1, keepdims=True)
    code = jnp.where(slot_row >= 0, iota((slots, 1), 0) // SLOTS * rows + slot_row, -1)
    select = jnp.concatenate(
        [ones(group[q : q + 1] * rows + row[q : q + 1] == code) for q in range(lines)], axis=1
    )
    lane = iota((slots, LANES), 1)
    mark = (lane // 16 == me_ref[0] // 2 % 8) & (lane % SLOTS == iota((slots, LANES), 0) % SLOTS)
    mark = jnp.where(mark, (slot_row + 1).astype(jnp.float32), 0.0)
    top = iota((slots, LANES), 0) % TILE < SLOTS
    pairs = groups // 2
    sums = {blocks: mark}
    tiles = {}

    def tile(low, high):
        return jnp.where(top, low, high).reshape(pairs, TILE, LANES)

    def up(x):
        return pltpu.roll(x, slots - SLOTS, 0)

    def store(t):
        both = jnp.concatenate([tiles.pop(t), tiles.pop(t + 1)], axis=1)
        out_ref[:, t * TILE : (t + 2) * TILE, :] = both.astype(jnp.bfloat16)

    for c in range(0, blocks, 2):
        part = jnp.concatenate(
            [came_ref[:, i * cap : (i + 1) * cap, :].reshape(locs * cap, LANES) for i in (c, c + 1)], axis=1
        )
        part = dot(select, part)
        sums[c], sums[c + 1] = part[:, :LANES], part[:, LANES:]
        tiles[c // 2] = tile(sums[c], pltpu.roll(sums[c + 1], SLOTS, 0))
        tiles[blocks // 2 + c // 2] = tile(up(sums[c - 1]), sums[c]) if c else tile(mark, sums[0])
        if c % 4 == 2:
            store(c // 2 - 1)
            store(blocks // 2 + c // 2 - 1)
    out_ref[:, blocks * TILE :, :] = tile(up(sums[blocks - 1]), mark).astype(jnp.bfloat16)


def update_kernel(landed_ref, table_ref, first_ref, second_ref, t_to, f_to, s_to, t_out, f_out, s_out, sem):
    pairs = landed_ref.shape[0]
    rows, width = table_ref.shape
    blocks = width // LANES
    lines = pairs // 8
    shape = (lines, pairs * TILE)
    source, line = iota(shape, 1) // TILE // 8, iota(shape, 0)
    target = iota((4 * rows, LANES), 0) % rows
    same_block = iota((4 * rows, LANES), 0) // rows == iota((4 * rows, LANES), 1) % 16 // SLOTS
    members = []
    for at, last in ((blocks // 2 * TILE, False), (blocks * TILE, True)):
        tags = landed_ref[:, at : at + TILE, :].astype(jnp.float32).reshape(pairs * TILE, LANES)
        low = iota(shape, 1) % TILE < SLOTS
        pick = ones((source == line) & (jnp.logical_not(low) if last else low))
        tags = dot(pick, tags.astype(jnp.bfloat16)).astype(jnp.int32) - 1
        members.append(
            jnp.concatenate([ones((tags[i : i + 1] == target) & same_block) for i in range(lines)], axis=1)
        )
    found = members[0][:rows].astype(jnp.float32) + members[1][:rows].astype(jnp.float32)
    touched = jnp.max(found, axis=1, keepdims=True) > 0.5
    halves = []
    for t in range(0, blocks, 4):
        part = [
            landed_ref[:, i * TILE : (i + 2) * TILE, :].reshape(pairs * 2 * TILE, LANES) for i in (t, t + 2)
        ]
        part = dot(members[t >= blocks // 2], jnp.concatenate(part, axis=1))
        for i in range(8):
            halves.append(part[i % 4 * rows : (i % 4 + 1) * rows, i // 4 * LANES : (i // 4 + 1) * LANES])
    end = landed_ref[:, blocks * TILE :, :].astype(jnp.float32)
    end = jnp.concatenate([end, jnp.zeros_like(end)], axis=1).reshape(pairs * 2 * TILE, LANES)
    halves.append(dot(members[1][:rows], end.astype(jnp.bfloat16)))
    corr_one = 1.0 - beta_one**ADAM_STEP
    corr_two = 1.0 - beta_two**ADAM_STEP
    writes = []
    for c in range(blocks):
        grad = halves[c] + halves[blocks + 1 + c]
        at = slice(c * LANES, (c + 1) * LANES)
        first, second, table = first_ref[:, at], second_ref[:, at], table_ref[:, at]
        first_next = beta_one * first + (1.0 - beta_one) * grad
        second_next = beta_two * second + (1.0 - beta_two) * grad * grad
        update = learn_rate * (first_next / corr_one) / (jnp.sqrt(second_next / corr_two) + epsilon)
        t_out[:, at] = jnp.where(touched, table - update, table)
        f_out[:, at] = jnp.where(touched, first_next, first)
        s_out[:, at] = jnp.where(touched, second_next, second)
        if (c + 1) % (blocks // 2) == 0:
            done = pl.ds((c + 1 - blocks // 2) * LANES, blocks // 2 * LANES)
            for a, b in ((t_out, t_to), (f_out, f_to), (s_out, s_to)):
                writes.append(pltpu.make_async_copy(a.at[:, done], b.at[:, done], sem.at[len(writes)]))
                writes[-1].start()
    for write in writes:
        write.wait()


PARAMS = pltpu.CompilerParams(vmem_limit_bytes=32 << 20)
WIDE = pltpu.CompilerParams(vmem_limit_bytes=60 << 20)


def pack(me, dest, group, row, grads, locs, cap, side):
    width = grads.shape[1]
    shape = (locs, width // LANES * cap + TAG_ONE, LANES)
    return pl.pallas_call(
        functools.partial(pack_kernel, locs, cap, side),
        out_shape=jax.ShapeDtypeStruct(shape, jnp.bfloat16),
        in_specs=[SMEM, ANY, ANY, ANY, ANY],
        out_specs=ANY,
        scratch_shapes=[
            pltpu.VMEM(dest.shape, jnp.int32),
            pltpu.VMEM(group.shape, jnp.int32),
            pltpu.VMEM(row.shape, jnp.int32),
            pltpu.VMEM(grads.shape, jnp.bfloat16),
            pltpu.VMEM(shape, jnp.bfloat16),
            pltpu.SemaphoreType.DMA((4 + PARTS,)),
        ],
        compiler_params=WIDE,
    )(me, dest, group, row, grads)


def combine(me, came, groups, rows, cap):
    blocks = (came.shape[1] - TAG_ONE) // cap
    shape = (groups // 2, (blocks + 1) * TILE, LANES)
    return pl.pallas_call(
        functools.partial(combine_kernel, groups, rows, cap),
        out_shape=jax.ShapeDtypeStruct(shape, jnp.bfloat16),
        in_specs=[SMEM, VMEM],
        out_specs=VMEM,
        compiler_params=PARAMS,
    )(me, came)


def update(landed, table, first, second):
    return pl.pallas_call(
        update_kernel,
        out_shape=(jax.ShapeDtypeStruct(table.shape, table.dtype),) * 3,
        in_specs=[VMEM] * 4,
        out_specs=(ANY,) * 3,
        scratch_shapes=[pltpu.VMEM(table.shape, table.dtype)] * 3 + [pltpu.SemaphoreType.DMA((6,))],
        compiler_params=PARAMS,
    )(landed, table, first, second)


def per_device(
    token_grads, owner_loc, owner_group, owner_row, embed_table, first_moment, second_moment
):
    locs = lax.axis_size("loc")
    groups = lax.axis_size("grp")
    rows = embed_table.shape[0]
    cap = 4 * token_grads.shape[0] // locs
    at_loc = loc_place(lax.axis_index("loc").astype(jnp.int32), locs).reshape(1)
    loc_order = sorted(range(locs), key=lambda loc: loc_place(loc, locs))
    side = math.isqrt(groups)
    at_group = group_place(lax.axis_index("grp").astype(jnp.int32), side).reshape(1)
    group_order = [group_place(g, side) for g in range(groups)]
    packed = pack(at_loc, owner_loc.T, owner_group.T, owner_row.T, token_grads, locs, cap, side)
    came = lax.all_to_all(
        packed, "loc", split_axis=0, concat_axis=0, tiled=True, axis_index_groups=[loc_order]
    )
    sums = combine(at_group, came, groups, rows, cap)
    shape = sums.shape
    sums = sums.reshape(groups, shape[1] // TILE, SLOTS, LANES)
    landed = lax.all_to_all(
        sums, "grp", split_axis=0, concat_axis=0, tiled=True, axis_index_groups=[group_order]
    ).reshape(shape)
    return tuple(update(landed, embed_table, first_moment, second_moment))


def solution(mesh):
    rows = P(("grp", "loc"), None)
    return jax.shard_map(
        per_device, mesh=mesh, in_specs=(rows,) * 7, out_specs=(rows,) * 3, check_vma=False
    )
```
